128 devices in a mesh: dp: 32 (over x, z, core), mp: 4 (over y).
Axes of the slice: x: 4, y: 4, z: 4, core: 2. Of those that a mesh axis runs over, the one named last changes fastest.
Arguments:
- preactivation: bfloat16 [14336, 32768], P('dp', 'mp'), may hold values from -6 to 6
- upstream: bfloat16 [14336, 512], P('dp'), may hold values from -0.29882812 to 0.29882812
- weight: bfloat16 [32768, 512], P('mp'), may hold values from -40 to 40
- first_moment: float32 [32768, 512], P(('mp', 'dp')), may hold values from -4 to 4
- second_moment: float32 [32768, 512], P(('mp', 'dp')), may hold values from 1 to 16
Outputs:
- input_grad: bfloat16 [14336, 32768], P('dp', 'mp')
- new_weight: bfloat16 [32768, 512], P('mp')
- first_next: float32 [32768, 512], P(('mp', 'dp'))
- second_next: float32 [32768, 512], P(('mp', 'dp'))
- trust_step: float32 [32768, 512], P(('mp', 'dp'))
The draws below stay inside these ranges and needn't reach their ends.
All inputs are finite; a program needn't handle non-finite values.
Results may differ from the reference program's by a relative error of at most 0.015.
Values may be sent and summed in bfloat16 or wider, within the bound.
No kernel may reach another device: no remote copies, remote signals or barrier semaphores. Data moves between devices by JAX's collectives and lax.ppermute only.
A program may use at most 128 MiB of HBM per device.

```python
import math
import jax
import jax.numpy as jnp
from jax import lax

D = 512
FF = 32768
TOK_DEV = 448
STEP = 1000
TOKENS = 14336
N_DP = 32


def draw_weight(key, part):
    key = jax.random.fold_in(key, 11)
    key_base, key_rows, key_cols = jax.random.split(key, 3)
    position = jnp.arange(FF, dtype=jnp.float32) / (FF - 1)
    base = jax.random.truncated_normal(key_base, -4.0, 4.0, (FF, D), jnp.float32)
    rising = 3.0 ** (0.5 * position)
    row_spread = jnp.exp(jax.random.uniform(key_rows, (FF, 1), jnp.float32, -1.15, 1.15))
    col_spread = jnp.exp(jax.random.uniform(key_cols, (1, D), jnp.float32, -0.5, 0.5))
    return (base * rising[:, None] * row_spread * col_spread).astype(jnp.bfloat16)


def with_spikes(values, key, source, target, parts, factor):
    owner, partner = [(jnp.arange(values.shape[dim]) // (values.shape[dim] // parts)).reshape([-1 if axis == dim else 1 for axis in range(values.ndim)]) for dim in (source, target)]
    chosen = jax.random.permutation(key, parts)[partner]
    strong = (owner == chosen) | (owner == (partner + parts // 2) % parts)
    return jnp.where(strong, factor * values, values)


def steps_of(stream_key, extent, cuts, smallest, largest):
    def one(dim, shards_of):
        draws = jax.random.uniform(jax.random.fold_in(jax.random.fold_in(stream_key, 6), dim), (shards_of,), jnp.float32, smallest / len(cuts), largest / len(cuts))
        return jnp.repeat(jnp.exp(draws), extent[dim] // shards_of).reshape((-1,) + (1,) * (len(extent) - dim - 1))

    factor_of = one(*cuts[0])
    for cut in cuts[1:]:
        factor_of = factor_of * one(*cut)
    return factor_of


def noise(rng, dims, scale, bound, cuts=(), kind=jnp.bfloat16):
    values = scale * jax.random.normal(rng, dims, jnp.float32)
    if cuts:
        values = values * steps_of(rng, dims, cuts, -0.22, 0.18)
    return jnp.clip(values, -bound, bound).astype(kind)


def noise_with(own_key, extent, width, reach, cuts, heavy, kind=jnp.bfloat16):
    values = width * jax.random.normal(own_key, extent, jnp.float32)
    if cuts:
        values = values * steps_of(own_key, extent, cuts, -0.22, 0.18)
    return jnp.clip(with_spikes(values, jax.random.fold_in(own_key, 3), *heavy), -reach, reach).astype(kind)


def setup_inputs(seed: int = 0) -> dict:
    key_of = jax.random.split(jax.random.key(seed), 6)
    preactivation = noise_with(key_of[0], (TOKENS, FF), 1.0, 6.0, ((0, 32), (1, 4)), (0, 1, 32, 2.75))
    upstream = noise(key_of[1], (TOKENS, D), 0.044, 0.29882812, ((0, 32),))
    weight = draw_weight(jax.random.fold_in(key_of[5], 71), 0)
    first_moment = noise(key_of[3], (FF, D), 0.5, 4.0, ((0, 128),), jnp.float32)
    second_moment = jnp.clip(jnp.exp(math.log(16.0) - 2.7725887 * jax.random.uniform(key_of[4], (FF, D), jnp.float32) ** steps_of(key_of[4], (FF, D), ((0, 128),), -0.2, 0.2)), 1.0, 16.0)
    return dict(preactivation=preactivation, upstream=upstream, weight=weight, first_moment=first_moment, second_moment=second_moment)


def reference(preactivation, upstream, weight, first_moment, second_moment):
    hidden = jnp.maximum(preactivation, jnp.zeros((), jnp.bfloat16))
    pre_blocks = preactivation.reshape(N_DP, TOK_DEV, FF)
    hid_blocks = hidden.reshape(N_DP, TOK_DEV, FF)
    up_blocks = upstream.reshape(N_DP, TOK_DEV, D)

    def one_block(total, items):
        pre_block, hid_block, up_block = items
        back = jnp.dot(up_block, weight.T, preferred_element_type=jnp.float32)
        grad_block = jnp.where(pre_block > 0, back, jnp.zeros((), jnp.float32)).astype(jnp.bfloat16)
        partial_value = jnp.dot(hid_block.T, up_block, preferred_element_type=jnp.float32).astype(jnp.bfloat16)
        partial_value = lax.optimization_barrier(partial_value)
        return (total + partial_value.astype(jnp.float32), grad_block)
    gradient, grad_blocks = lax.scan(one_block, jnp.zeros((FF, D), jnp.float32), (pre_blocks, hid_blocks, up_blocks))
    input_grad = grad_blocks.reshape(N_DP * TOK_DEV, FF)
    beta_one = 0.9
    beta_two = 0.999
    bias_one = 1.0 - beta_one ** STEP
    bias_two = 1.0 - beta_two ** STEP
    first_next = beta_one * first_moment + (1.0 - beta_one) * gradient
    second_next = beta_two * second_moment + (1.0 - beta_two) * gradient * gradient
    weight_full = weight.astype(jnp.float32)
    update = first_next / bias_one / (jnp.sqrt(second_next / bias_two) + 1e-06) + 0.02 * weight_full
    weight_sq = jnp.sum(weight_full * weight_full)
    update_sq = jnp.sum(update * update)
    trust_step = jnp.sqrt(weight_sq) / jnp.sqrt(update_sq) * update
    new_weight = (weight_full - 0.02 * trust_step).astype(jnp.bfloat16)
    return (input_grad, new_weight, first_next, second_next, trust_step)
```

```python
import jax
import jax.numpy as jnp
from jax import lax
from jax.experimental import pallas as pl
from jax.experimental.pallas import tpu as pltpu
from jax.sharding import Mesh
from jax.sharding import PartitionSpec as P

STEP = 1000
DP = ("x", "z", "c")
ROWS = 256
D = 512


def shift_first(k):
    pairs = []
    for x in range(4):
        for z in range(4):
            pairs.append(((x * 4 + z) * 2, (((x + k) % 4) * 4 + z) * 2))
            pairs.append(((x * 4 + z) * 2 + 1, (x * 4 + (z + k) % 4) * 2 + 1))
    return pairs


def shift_second(k):
    pairs = []
    for x in range(4):
        for z in range(4):
            pairs.append(((x * 4 + z) * 2, (x * 4 + (z + k) % 4) * 2))
            pairs.append(((x * 4 + z) * 2 + 1, (((x + k) % 4) * 4 + z) * 2 + 1))
    return pairs


def along_first(value, k):
    return lax.ppermute(value, DP, shift_first(k))


def along_second(value, k):
    return lax.ppermute(value, DP, shift_second(k))


def along_y(value, k):
    return lax.ppermute(value, "y", [(i, (i + k) % 4) for i in range(4)])


def sibling(value):
    return lax.ppermute(value, "c", [(0, 1), (1, 0)])


def partial_body(blocks, own_ref, other_ref, up_ref, keep_ref, send_ref, up_t):
    @pl.when(pl.program_id(0) == 0)
    def _():
        up_t[...] = up_ref[...].T

    zero = jnp.zeros((), jnp.bfloat16)
    for source, target in ((own_ref, keep_ref), (other_ref, send_ref)):
        target[...] = jnp.dot(
            up_t[...], jnp.maximum(source[...], zero), preferred_element_type=jnp.float32
        ).astype(jnp.bfloat16)


def partial_terms(preactivation, upstream, own, other):
    count = own.shape[0]
    tokens = preactivation.shape[0]
    stacked = jax.ShapeDtypeStruct((count * D, ROWS), jnp.bfloat16)
    return pl.pallas_call(
        partial_body,
        out_shape=(stacked, stacked),
        grid_spec=pltpu.PrefetchScalarGridSpec(
            num_scalar_prefetch=1,
            grid=(count,),
            in_specs=[
                pl.BlockSpec((tokens, ROWS), lambda i, b: (0, b[i])),
                pl.BlockSpec((tokens, ROWS), lambda i, b: (0, b[count + i])),
                pl.BlockSpec((tokens, D), lambda i, b: (0, 0)),
            ],
            out_specs=[
                pl.BlockSpec((D, ROWS), lambda i, b: (i, 0)),
                pl.BlockSpec((D, ROWS), lambda i, b: (i, 0)),
            ],
            scratch_shapes=[pltpu.VMEM((D, tokens), jnp.bfloat16)],
        ),
        compiler_params=pltpu.CompilerParams(vmem_limit_bytes=16 * 2**20),
        cost_estimate=pl.CostEstimate(
            flops=4 * count * ROWS * D * tokens,
            bytes_accessed=4 * count * ROWS * (D + tokens),
            transcendentals=0,
        ),
        name="partial_terms",
    )(jnp.concatenate([own, other]), preactivation, preactivation, upstream)


def update_body(
    block, g0, g1, g2, g3, g4, g5, g6, first, second, weight,
    first_out, second_out, update_out, short_out, sums_out,
):
    beta_one = 0.9
    beta_two = 0.999
    bias_one = 1.0 - beta_one**STEP
    bias_two = 1.0 - beta_two**STEP
    total = g0[...].astype(jnp.float32)
    for ref in (g1, g2, g3, g4, g5, g6):
        total = total + ref[...].astype(jnp.float32)
    gradient = total.T
    own_weight = weight[...].astype(jnp.float32)
    first_next = beta_one * first[...] + (1.0 - beta_one) * gradient
    second_next = beta_two * second[...] + (1.0 - beta_two) * gradient * gradient
    update = first_next / bias_one / (jnp.sqrt(second_next / bias_two) + 1e-06) + 0.02 * own_weight
    first_out[...] = first_next
    second_out[...] = second_next
    update_out[...] = update
    short_out[...] = update.astype(jnp.bfloat16)
    update_sq = jnp.sum(update * update)
    weight_sq = jnp.sum(own_weight * own_weight)
    row = lax.broadcasted_iota(jnp.int32, (8, 128), 0)
    sums = jnp.where(row == 0, update_sq, weight_sq)

    @pl.when(pl.program_id(0) == 0)
    def _():
        sums_out[...] = sums

    @pl.when(pl.program_id(0) > 0)
    def _():
        sums_out[...] += sums


def update_rows(block, terms, first, second, weight):
    half = D // 2
    long = jax.ShapeDtypeStruct((ROWS, D), jnp.float32)
    rows = pl.BlockSpec((ROWS, half), lambda j, b: (0, j))
    return pl.pallas_call(
        update_body,
        out_shape=(
            long,
            long,
            long,
            jax.ShapeDtypeStruct((ROWS, D), jnp.bfloat16),
            jax.ShapeDtypeStruct((8, 128), jnp.float32),
        ),
        grid_spec=pltpu.PrefetchScalarGridSpec(
            num_scalar_prefetch=1,
            grid=(2,),
            in_specs=[pl.BlockSpec((half, ROWS), lambda j, b: (j, 0))] * 7
            + [rows, rows, pl.BlockSpec((ROWS, half), lambda j, b: (b[0], j))],
            out_specs=[rows, rows, rows, rows, pl.BlockSpec((8, 128), lambda j, b: (0, 0))],
        ),
        compiler_params=pltpu.CompilerParams(vmem_limit_bytes=24 * 2**20),
        cost_estimate=pl.CostEstimate(
            flops=20 * ROWS * D, bytes_accessed=38 * ROWS * D, transcendentals=ROWS * D
        ),
        name="update_rows",
    )(block.reshape(1), *terms, first, second, weight)


def apply_body(sizes, blocks, step_ref, weight, *refs):
    out = refs[-1]
    i = pl.program_id(0)
    begin = 0
    for size, ref in zip(sizes, refs[: len(sizes)]):

        @pl.when((i >= begin) & (i < begin + size))
        def _(ref=ref):
            out[...] = (
                weight[...].astype(jnp.float32) - step_ref[0, 0] * ref[...].astype(jnp.float32)
            ).astype(jnp.bfloat16)

        begin += size


def apply_update(blocks, step, weight, updates, before):
    sizes = [u.shape[0] // ROWS for u in updates]
    count = sum(sizes)
    specs = []
    begin = 0
    for size in sizes:
        specs.append(
            pl.BlockSpec(
                (ROWS, D),
                lambda i, b, begin=begin, size=size: (jnp.clip(i - begin, 0, size - 1), 0),
            )
        )
        begin += size
    extra = [] if before is None else [before]

    def body(blocks, *refs):
        apply_body(sizes, blocks, *refs)

    return pl.pallas_call(
        body,
        out_shape=jax.ShapeDtypeStruct(weight.shape, jnp.bfloat16),
        grid_spec=pltpu.PrefetchScalarGridSpec(
            num_scalar_prefetch=1,
            grid=(count,),
            in_specs=[
                pl.BlockSpec(memory_space=pltpu.SMEM),
                pl.BlockSpec((ROWS, D), lambda i, b: (b[i], 0)),
            ]
            + specs
            + [pl.BlockSpec(memory_space=pl.ANY)] * len(extra),
            out_specs=pl.BlockSpec((ROWS, D), lambda i, b: (b[i], 0)),
        ),
        input_output_aliases={} if before is None else {3 + len(updates): 0},
        compiler_params=pltpu.CompilerParams(vmem_limit_bytes=16 * 2**20),
        cost_estimate=pl.CostEstimate(
            flops=2 * count * ROWS * D, bytes_accessed=6 * count * ROWS * D, transcendentals=0
        ),
        name="apply_update",
    )(blocks, step, weight, *updates, *extra)


def added(*values):
    total = values[0].astype(jnp.float32)
    for value in values[1:]:
        total = total + value.astype(jnp.float32)
    return total.astype(jnp.bfloat16)


def per_device(preactivation, upstream, weight, first_moment, second_moment):
    x, z, c = lax.axis_index("x"), lax.axis_index("z"), lax.axis_index("c")
    first = jnp.where(c == 0, x, z)
    second = jnp.where(c == 0, z, x)
    first_stride = jnp.where(c == 0, 8, 2)
    second_stride = jnp.where(c == 0, 2, 8)
    four = jnp.arange(4, dtype=jnp.int32)

    def own_unit(k):
        return (first + k) % 4 * first_stride + (second + four) % 4 * second_stride + c

    def other_unit(k):
        return (second + k) % 4 * second_stride + (first + four) % 4 * first_stride + 1 - c

    keep_far, send_far = partial_terms(preactivation, upstream, own_unit(2), other_unit(2))
    far = added(keep_far, sibling(send_far))
    half = 2 * D
    from_left = along_first(far[:half], 1)
    from_right = along_first(far[half:], -1)

    keep_near, send_near = partial_terms(
        preactivation,
        upstream,
        jnp.concatenate([own_unit(1), own_unit(-1)]),
        jnp.concatenate([other_unit(1), other_unit(-1)]),
    )
    got_near = sibling(send_near)
    unit = 4 * D
    right = jnp.concatenate(
        [
            added(keep_near[:half], got_near[:half], from_left),
            added(keep_near[half:unit], got_near[half:unit]),
        ]
    )
    left = jnp.concatenate(
        [
            added(keep_near[unit : unit + half], got_near[unit : unit + half]),
            added(keep_near[unit + half :], got_near[unit + half :], from_right),
        ]
    )
    sum_left = along_first(right, 1)
    sum_right = along_first(left, -1)

    keep_here, send_here = partial_terms(preactivation, upstream, own_unit(0), other_unit(0))
    got_here = sibling(send_here)
    terms = [
        along_second(
            added(*(v[j * D : (j + 1) * D] for v in (keep_here, got_here, sum_left, sum_right))), j
        )
        for j in (1, 2, 3)
    ]

    back = lax.dot_general(
        upstream, weight, (((1,), (1,)), ((), ())), preferred_element_type=jnp.float32
    )
    input_grad = jnp.where(preactivation > 0, back, jnp.zeros((), jnp.float32)).astype(jnp.bfloat16)

    first_next, second_next, update, short, sums = update_rows(
        own_unit(0)[0],
        [keep_here, got_here, sum_left, sum_right, *terms],
        first_moment,
        second_moment,
        weight,
    )

    sums = sums + sibling(sums)
    sums = sums + along_y(sums, 1) + along_y(sums, 2) + along_y(sums, 3)
    sums = sums + along_second(sums, 1) + along_second(sums, 2) + along_second(sums, 3)
    sums = sums + along_first(sums, 1) + along_first(sums, 2) + along_first(sums, 3)
    ratio = jnp.sqrt(sums[1, 0]) / jnp.sqrt(sums[0, 0])
    trust_step = ratio * update
    step = (0.02 * ratio).reshape(1, 1)

    here = jnp.concatenate([short, *(along_second(short, -j) for j in (1, 2, 3))])
    near_left = along_first(here, 1)
    near_right = along_first(here, -1)
    far_left = along_first(near_left[: 2 * ROWS], 1)
    far_right = along_first(near_right[2 * ROWS :], -1)
    new_weight = apply_update(
        jnp.concatenate(
            [own_unit(0), other_unit(0), own_unit(-1), own_unit(1), other_unit(-1), other_unit(1)]
        ),
        step,
        weight,
        [here, sibling(here), near_left, near_right, sibling(near_left), sibling(near_right)],
        None,
    )
    new_weight = apply_update(
        jnp.concatenate([own_unit(2), other_unit(2)]),
        step,
        weight,
        [far_left, far_right, sibling(far_left), sibling(far_right)],
        new_weight,
    )
    return (input_grad, new_weight, first_next, second_next, trust_step)


def solution(mesh):
    split = Mesh(mesh.devices.reshape(4, 4, 2, 4), ("x", "z", "c", "y"))
    rows = P(("y", "x", "z", "c"), None)
    return jax.shard_map(
        per_device,
        mesh=split,
        in_specs=(P(DP, "y"), P(DP, None), P("y", None), rows, rows),
        out_specs=(P(DP, "y"), P("y", None), rows, rows, rows),
        check_vma=False,
    )
```

```python
import jax
import jax.numpy as jnp
from jax import lax
from jax.experimental import pallas as pl
from jax.experimental.pallas import tpu as pltpu
from jax.sharding import Mesh
from jax.sharding import PartitionSpec as P

STEP = 1000
DP = ("x", "z", "c")
ROWS = 256
D = 512
VMEM = pl.BlockSpec(memory_space=pltpu.VMEM)
SMEM = pl.BlockSpec(memory_space=pltpu.SMEM)
HBM = pl.BlockSpec(memory_space=pltpu.HBM)
SHORT = pl.CostEstimate(flops=2**20, bytes_accessed=2**16, transcendentals=0)
LONG = pl.CostEstimate(flops=2**34, bytes_accessed=2**26, transcendentals=0)


def shift_first(k):
    pairs = []
    for x in range(4):
        for z in range(4):
            pairs.append(((x * 4 + z) * 2, (((x + k) % 4) * 4 + z) * 2))
            pairs.append(((x * 4 + z) * 2 + 1, (x * 4 + (z + k) % 4) * 2 + 1))
    return pairs


def shift_second(k):
    pairs = []
    for x in range(4):
        for z in range(4):
            pairs.append(((x * 4 + z) * 2, (x * 4 + (z + k) % 4) * 2))
            pairs.append(((x * 4 + z) * 2 + 1, (((x + k) % 4) * 4 + z) * 2 + 1))
    return pairs


def along_first(value, k):
    return lax.ppermute(value, DP, shift_first(k))


def along_second(value, k):
    return lax.ppermute(value, DP, shift_second(k))


def paired(value, axes, turn):
    pairs = ((1, 0, 3, 2), (3, 2, 1, 0))[turn]
    if axes == "y":
        return value + lax.ppermute(value, "y", list(enumerate(pairs)))
    moves = []
    for x in range(4):
        for z in range(4):
            for c in range(2):
                along_x = (axes == "first") == (c == 0)
                nx, nz = (pairs[x], z) if along_x else (x, pairs[z])
                moves.append(((x * 4 + z) * 2 + c, (nx * 4 + nz) * 2 + c))
    return value + lax.ppermute(value, DP, moves)


def summed(value, axes):
    return paired(paired(value, axes, 0), axes, 1)


def sibling(value):
    return lax.ppermute(value, "c", [(0, 1), (1, 0)])


def in_hbm(value):
    return pltpu.with_memory_space_constraint(value, pltpu.HBM)


def in_vmem(value):
    return pltpu.with_memory_space_constraint(value, pltpu.VMEM)


def after(value, *others):
    return lax.optimization_barrier((value, *others))[0]


def first_body(picks, blocks, up_ref, pre_ref, out, up_t, columns, arrived, up, up_arrived):
    copies = []
    up_copy = pltpu.make_async_copy(up_ref, up, up_arrived)
    up_copy.start()
    for i, pick in enumerate(picks):
        start = pl.multiple_of(blocks[pick] * ROWS, ROWS)
        copies.append(
            pltpu.make_async_copy(
                pre_ref.at[:, pl.ds(start, ROWS)],
                columns.at[:, pl.ds(i * ROWS, ROWS)],
                arrived.at[i],
            )
        )
        copies[-1].start()
    up_copy.wait()
    up_t[...] = up[...].T
    zero = jnp.zeros((), jnp.bfloat16)
    for i, copy in enumerate(copies):
        copy.wait()
        out[i * D : (i + 1) * D, :] = jnp.dot(
            up_t[...],
            jnp.maximum(columns[:, i * ROWS : (i + 1) * ROWS], zero),
            preferred_element_type=jnp.float32,
        ).astype(jnp.bfloat16)


def first_terms(preactivation, upstream, blocks, picks):
    tokens = preactivation.shape[0]

    def body(*refs):
        first_body(picks, *refs)

    return pl.pallas_call(
        body,
        out_shape=(
            jax.ShapeDtypeStruct((len(picks) * D, ROWS), jnp.bfloat16),
            jax.ShapeDtypeStruct((D, tokens), jnp.bfloat16),
        ),
        in_specs=[SMEM, HBM, HBM],
        out_specs=(VMEM, VMEM),
        scratch_shapes=[
            pltpu.VMEM((tokens, len(picks) * ROWS), jnp.bfloat16),
            pltpu.SemaphoreType.DMA((len(picks),)),
            pltpu.VMEM(upstream.shape, upstream.dtype),
            pltpu.SemaphoreType.DMA,
        ],
        compiler_params=pltpu.CompilerParams(vmem_limit_bytes=16 * 2**20),
        cost_estimate=LONG,
        name="first_terms",
    )(blocks, in_hbm(upstream), in_hbm(preactivation))


def terms_body(picks, parts, adds, blocks, up_ref, pre_ref, *refs):
    ins, outs = refs[: sum(map(len, adds))], refs[sum(map(len, adds)) :]
    zero = jnp.zeros((), jnp.bfloat16)
    picks = list(picks)
    for part, offsets, out in zip(parts, adds, outs):
        mine, ins = ins[: len(offsets)], ins[len(offsets) :]
        for k in range(part):
            start = pl.multiple_of(blocks[picks.pop(0)] * ROWS, ROWS)
            total = jnp.dot(
                up_ref[...],
                jnp.maximum(pre_ref[:, pl.ds(start, ROWS)], zero),
                preferred_element_type=jnp.float32,
            )
            for ref, offset in zip(mine, offsets):
                begin = offset + k * D
                total = total + ref[begin : begin + D, :].astype(jnp.float32)
            out[k * D : (k + 1) * D, :] = total.astype(jnp.bfloat16)


def terms(preactivation, up_t, blocks, picks, parts, adds=None, cost=SHORT):
    adds = adds or [()] * len(parts)
    offsets = [[begin for _, begin in group] for group in adds]

    def body(*refs):
        terms_body(picks, parts, offsets, *refs)

    return pl.pallas_call(
        body,
        out_shape=tuple(jax.ShapeDtypeStruct((p * D, ROWS), jnp.bfloat16) for p in parts),
        in_specs=[SMEM, VMEM, VMEM] + [VMEM] * sum(map(len, adds)),
        out_specs=tuple(VMEM for _ in parts),
        compiler_params=pltpu.CompilerParams(vmem_limit_bytes=16 * 2**20),
        cost_estimate=cost,
        name="terms",
    )(blocks, up_t, in_vmem(preactivation), *(a for group in adds for a, _ in group))


WIDE = 2048


def back_body(lo, count, tokens, up_ref, pre_ref, weight_ref, *refs):
    def step(weight, out):
        back = lax.dot_general(
            up_ref[...], weight[...], (((1,), (1,)), ((), ())), preferred_element_type=jnp.float32
        )
        start = pl.multiple_of((pl.program_id(0) + lo) * WIDE, WIDE)
        out[...] = jnp.where(
            pre_ref[:, pl.ds(start, WIDE)] > 0,
            back.astype(jnp.bfloat16),
            jnp.zeros((), jnp.bfloat16),
        )

    step(weight_ref, refs[-1])


def back_columns(lo, count, upstream, preactivation, weight, before):
    extra = [] if before is None else [before]
    tokens = preactivation.shape[0]

    def body(*refs):
        back_body(lo, count, tokens, *refs)

    return pl.pallas_call(
        body,
        out_shape=jax.ShapeDtypeStruct(preactivation.shape, jnp.bfloat16),
        grid=(count,),
        in_specs=[VMEM, VMEM, pl.BlockSpec((WIDE, D), lambda i: (i + lo, 0))]
        + [pl.BlockSpec(memory_space=pl.ANY)] * len(extra),
        out_specs=pl.BlockSpec((tokens, WIDE), lambda i: (0, i + lo)),
        input_output_aliases={3: 0} if extra else {},
        compiler_params=pltpu.CompilerParams(vmem_limit_bytes=24 * 2**20),
        cost_estimate=LONG,
        name="back_columns",
    )(upstream, in_vmem(preactivation), in_hbm(weight), *map(in_hbm, extra))


def update_body(
    block, g0, g1, g2, g3, g4, g5, first, second, weight,
    first_out, second_out, update_out, short_out, sums_out, own, arrived,
):
    beta_one = 0.9
    beta_two = 0.999
    bias_one = 1.0 - beta_one**STEP
    bias_two = 1.0 - beta_two**STEP
    start = pl.multiple_of(block[0] * ROWS, ROWS)
    fetch = pltpu.make_async_copy(weight.at[pl.ds(start, ROWS)], own, arrived)
    fetch.start()
    update_sq = jnp.zeros((8, 128), jnp.float32)
    weight_sq = jnp.zeros((8, 128), jnp.float32)
    for j in range(D // 128):
        part = slice(j * 128, (j + 1) * 128)
        total = g0[part, :].astype(jnp.float32)
        for ref in (g1, g2, g3, g4, g5):
            total = total + ref[part, :].astype(jnp.float32)
        gradient = total.T
        first_next = beta_one * first[:, part] + (1.0 - beta_one) * gradient
        second_next = beta_two * second[:, part] + (1.0 - beta_two) * gradient * gradient
        if j == 0:
            fetch.wait()
        own_weight = own[:, part].astype(jnp.float32)
        update = (
            first_next * (1.0 / bias_one) / (jnp.sqrt(second_next * (1.0 / bias_two)) + 1e-06)
            + 0.02 * own_weight
        )
        first_out[:, part] = first_next
        second_out[:, part] = second_next
        update_out[:, part] = update
        short_out[:, part] = update.astype(jnp.bfloat16)
        update_sq = update_sq + jnp.sum((update * update).reshape(ROWS // 8, 8, 128), axis=0)
        weight_sq = weight_sq + jnp.sum(
            (own_weight * own_weight).reshape(ROWS // 8, 8, 128), axis=0
        )
    sums_out[0:8, :] = update_sq
    sums_out[8:16, :] = weight_sq


def update_rows(block, parts, first, second, weight):
    long = jax.ShapeDtypeStruct((ROWS, D), jnp.float32)
    return pl.pallas_call(
        update_body,
        out_shape=(
            long,
            long,
            long,
            jax.ShapeDtypeStruct((ROWS, D), jnp.bfloat16),
            jax.ShapeDtypeStruct((16, 128), jnp.float32),
        ),
        in_specs=[SMEM]
        + [VMEM] * 6
        + [VMEM, VMEM, HBM],
        out_specs=(VMEM,) * 5,
        scratch_shapes=[pltpu.VMEM((ROWS, D), jnp.bfloat16), pltpu.SemaphoreType.DMA],
        compiler_params=pltpu.CompilerParams(vmem_limit_bytes=16 * 2**20),
        cost_estimate=SHORT,
        name="update_rows",
    )(block, *parts, first, second, in_hbm(weight))


def apply_body(picks, sizes, trust, blocks, sums_ref, weight, *refs):
    updates = refs[: len(sizes)]
    ready, stored = refs[-2:]
    if trust:
        update_ref, out, trust_out = refs[len(sizes)], refs[-4], refs[-3]
    else:
        out = refs[-3]
    update_sq = jnp.sum(sums_ref[0:8, :], axis=(0, 1), keepdims=True)
    weight_sq = jnp.sum(sums_ref[8:16, :], axis=(0, 1), keepdims=True)
    ratio = jnp.sqrt(weight_sq) / jnp.sqrt(update_sq)
    step = (0.02 * ratio).astype(jnp.bfloat16)
    places = [(update, k) for size, update in zip(sizes, updates) for k in range(size)]
    stores = []
    for i, (update, k) in enumerate(places):
        begin = pl.multiple_of(blocks[picks[i]] * ROWS, ROWS)
        ready[i] = weight[pl.ds(begin, ROWS), :] - step * update[k * ROWS : (k + 1) * ROWS, :]
        stores.append(
            pltpu.make_async_copy(ready.at[i], out.at[pl.ds(begin, ROWS)], stored.at[i])
        )
        stores[-1].start()
    if trust:
        trust_out[...] = ratio * update_ref[...]
    for store in stores:
        store.wait()


def apply_update(blocks, picks, sums, weight, updates, update, before):
    sizes = [u.shape[0] // ROWS for u in updates]
    count = sum(sizes)
    trust = [] if update is None else [update]
    extra = [] if before is None else [before]

    def body(*refs):
        apply_body(picks, sizes, bool(trust), *refs)

    return pl.pallas_call(
        body,
        out_shape=(jax.ShapeDtypeStruct(weight.shape, jnp.bfloat16),)
        + tuple(jax.ShapeDtypeStruct(u.shape, u.dtype) for u in trust),
        in_specs=[SMEM, VMEM, VMEM] + [VMEM] * (len(updates) + len(trust)) + [HBM] * len(extra),
        out_specs=(HBM,) + (VMEM,) * len(trust),
        input_output_aliases={3 + len(updates) + len(trust): 0} if extra else {},
        scratch_shapes=[
            pltpu.VMEM((count, ROWS, D), jnp.bfloat16),
            pltpu.SemaphoreType.DMA((count,)),
        ],
        compiler_params=pltpu.CompilerParams(vmem_limit_bytes=16 * 2**20),
        cost_estimate=SHORT,
        name="apply_update",
    )(blocks, sums, in_vmem(weight), *updates, *trust, *map(in_hbm, extra))


def joined(*values):
    rows = values[0].shape[0]

    def body(*refs):
        for k, ref in enumerate(refs[:-1]):
            refs[-1][k * rows : (k + 1) * rows, :] = ref[...]

    return pl.pallas_call(
        body,
        out_shape=jax.ShapeDtypeStruct((len(values) * rows, D), values[0].dtype),
        in_specs=[VMEM] * len(values),
        out_specs=VMEM,
        compiler_params=pltpu.CompilerParams(vmem_limit_bytes=16 * 2**20),
        cost_estimate=SHORT,
        name="joined",
    )(*values)


def taken(value, begin):
    rows = value.shape[0] // 2

    def body(ref, out):
        out[...] = ref[begin : begin + rows, :]

    return pl.pallas_call(
        body,
        out_shape=jax.ShapeDtypeStruct((rows, value.shape[1]), value.dtype),
        in_specs=[VMEM],
        out_specs=VMEM,
        compiler_params=pltpu.CompilerParams(vmem_limit_bytes=16 * 2**20),
        cost_estimate=SHORT,
        name="taken",
    )(value)


def added(*values):
    total = values[0].astype(jnp.float32)
    for value in values[1:]:
        total = total + value.astype(jnp.float32)
    return total.astype(jnp.bfloat16)


def own_unit(k):
    return [k % 4 * 4 + j for j in range(4)]


def other_unit(k):
    return [16 + k % 4 * 4 + j for j in range(4)]


def per_device(preactivation, upstream, weight, first_moment, second_moment):
    x, z, c = lax.axis_index("x"), lax.axis_index("z"), lax.axis_index("c")
    first = jnp.where(c == 0, x, z)
    second = jnp.where(c == 0, z, x)
    first_stride = jnp.where(c == 0, 8, 2)
    second_stride = jnp.where(c == 0, 2, 8)
    place = jnp.arange(32, dtype=jnp.int32)
    unit, member = (place >> 2) & 3, place & 3
    mine = place < 16
    on_first = (first + jnp.where(mine, unit, member)) & 3
    on_second = (second + jnp.where(mine, member, unit)) & 3
    blocks = on_first * first_stride + on_second * second_stride + jnp.where(mine, c, 1 - c)

    near_free = lambda unit: unit(1)[2:] + unit(-1)[:2]
    near_late = lambda unit: unit(1)[:2] + unit(-1)[2:]

    send_far, up_t = first_terms(preactivation, upstream, blocks, other_unit(2))

    def part(picks, parts, adds=None, then=(), cost=SHORT):
        return terms(preactivation, after(up_t, *then), blocks, picks, parts, adds, cost)

    got_far = sibling(send_far)
    keep_far = part(own_unit(2), (2, 2), then=(send_far,), cost=LONG)
    half = 2 * D
    (send_free,) = part(near_free(other_unit), (4,), then=keep_far)
    keep_far = [after(v, send_free) for v in keep_far]
    far_low = added(keep_far[0], got_far[:half])
    far_high = added(keep_far[1], got_far[half:])
    from_left = along_first(far_low, 1)
    from_right = along_first(far_high, -1)

    got_free = sibling(send_free)
    (send_late,) = part(near_late(other_unit), (4,), then=(far_low, far_high), cost=LONG)
    got_late = sibling(send_late)
    right_high, left_low = part(
        near_free(own_unit), (2, 2), [[(got_free, 0)], [(got_free, half)]], then=(send_late,)
    )
    sum_left_high = along_first(right_high, 1)
    sum_right_low = along_first(left_low, -1)
    (send_here,) = part(other_unit(0), (4,), then=(right_high, left_low), cost=LONG)
    got_here = sibling(send_here)
    right_low, left_high = part(
        near_late(own_unit),
        (2, 2),
        [[(got_late, 0), (from_left, 0)], [(got_late, half), (from_right, 0)]],
        then=(send_here,),
    )
    sum_left_low = along_first(right_low, 1)
    sum_right_high = along_first(left_high, -1)
    input_grad = back_columns(
        0, 2, after(upstream, right_low, left_high), preactivation, weight, None
    )
    (here,) = part(own_unit(0), (4,), [[(got_here, 0)]], then=(input_grad,))
    near = (
        added(here[D:half], sum_left_low[D:], sum_right_low[D:]),
        added(here[half : half + D], sum_left_high[:D], sum_right_high[:D]),
        added(here[half + D :], sum_left_high[D:], sum_right_high[D:]),
    )
    got = [along_second(v, j) for v, j in zip(near, (1, 2, 3))]
    input_grad = back_columns(2, 2, after(upstream, *near), preactivation, weight, input_grad)
    first_next, second_next, update, short, sums = update_rows(
        blocks,
        [here, sum_left_low, sum_right_low, *got],
        first_moment,
        second_moment,
        after(weight, input_grad),
    )

    rows = [along_second(short, -j) for j in (1, 2, 3)]
    sums = summed(sums, "first")
    mine = joined(after(short, sums), *rows)
    mine_other = sibling(mine)
    near_left = along_first(mine, 1)
    near_right = along_first(mine, -1)
    sums = paired(summed(after(sums, mine), "second"), "y", 0)
    near_left = after(near_left, sums, mine_other)
    near_right = after(near_right, sums, mine_other)
    low = taken(near_left, 0)
    high = taken(near_right, 2 * ROWS)
    far_left = along_first(low, 1)
    far_right = along_first(high, -1)
    near_left, near_right = after(near_left, low, high), after(near_right, low, high)
    sums = paired(after(sums, low, high), "y", 1)
    sums = sums + sibling(sums)
    far_left, far_right = after(far_left, sums), after(far_right, sums)
    new_weight, trust_step = apply_update(
        blocks,
        own_unit(0) + other_unit(0) + own_unit(-1) + own_unit(1) + other_unit(-1) + other_unit(1),
        sums,
        weight,
        [mine, mine_other, near_left, near_right, sibling(near_left), sibling(near_right)],
        update,
        None,
    )
    (new_weight,) = apply_update(
        blocks,
        own_unit(2) + other_unit(2),
        sums,
        weight,
        [far_left, far_right, sibling(far_left), sibling(far_right)],
        None,
        new_weight,
    )
    return (input_grad, new_weight, first_next, second_next, trust_step)


def solution(mesh):
    split = Mesh(mesh.devices.reshape(4, 4, 2, 4), ("x", "z", "c", "y"))
    rows = P(("y", "x", "z", "c"), None)
    return jax.shard_map(
        per_device,
        mesh=split,
        in_specs=(P(DP, "y"), P(DP, None), P("y", None), rows, rows),
        out_specs=(P(DP, "y"), P("y", None), rows, rows, rows),
        check_vma=False,
    )
```

```python
import jax
import jax.numpy as jnp
from jax import lax
from jax.experimental import pallas as pl
from jax.experimental.pallas import tpu as pltpu
from jax.sharding import Mesh
from jax.sharding import PartitionSpec as P

STEP = 1000
DP = ("x", "z", "c")
ROWS = 256
D = 512
VMEM = pl.BlockSpec(memory_space=pltpu.VMEM)
SMEM = pl.BlockSpec(memory_space=pltpu.SMEM)
HBM = pl.BlockSpec(memory_space=pltpu.HBM)
SHORT = pl.CostEstimate(flops=2**20, bytes_accessed=2**16, transcendentals=0)
LONG = pl.CostEstimate(flops=2**34, bytes_accessed=2**26, transcendentals=0)


def exchanges(axis, k):
    pairs = []
    for x in range(4):
        for z in range(4):
            for c in range(2):
                along_x = (axis == "first") == (c == 0)
                to_x, to_z = (x ^ k, z) if along_x else (x, z ^ k)
                pairs.append(((x * 4 + z) * 2 + c, (to_x * 4 + to_z) * 2 + c))
    return pairs


def along_first(value, k):
    return lax.ppermute(value, DP, exchanges("first", k))


def along_second(value, k):
    return lax.ppermute(value, DP, exchanges("second", k))


def along_y(value, k):
    return lax.ppermute(value, "y", [(y, y ^ k) for y in range(4)])


def sibling(value):
    return lax.ppermute(value, "c", [(0, 1), (1, 0)])


def in_hbm(value):
    return pltpu.with_memory_space_constraint(value, pltpu.HBM)


def in_vmem(value):
    return pltpu.with_memory_space_constraint(value, pltpu.VMEM)


def after(value, *others):
    return lax.optimization_barrier((value, *others))[0]


def first_body(picks, blocks, up_ref, pre_ref, out, up_t, columns, arrived, up, up_arrived):
    copies = []
    up_copy = pltpu.make_async_copy(up_ref, up, up_arrived)
    up_copy.start()
    for i, pick in enumerate(picks):
        start = pl.multiple_of(blocks[pick] * ROWS, ROWS)
        copies.append(
            pltpu.make_async_copy(
                pre_ref.at[:, pl.ds(start, ROWS)],
                columns.at[:, pl.ds(i * ROWS, ROWS)],
                arrived.at[i],
            )
        )
        copies[-1].start()
    up_copy.wait()
    up_t[...] = up[...].T
    zero = jnp.zeros((), jnp.bfloat16)
    for i, copy in enumerate(copies):
        copy.wait()
        out[i * D : (i + 1) * D, :] = jnp.dot(
            up_t[...],
            jnp.maximum(columns[:, i * ROWS : (i + 1) * ROWS], zero),
            preferred_element_type=jnp.float32,
        ).astype(jnp.bfloat16)


def first_terms(preactivation, upstream, blocks, picks):
    tokens = preactivation.shape[0]

    def body(*refs):
        first_body(picks, *refs)

    return pl.pallas_call(
        body,
        out_shape=(
            jax.ShapeDtypeStruct((len(picks) * D, ROWS), jnp.bfloat16),
            jax.ShapeDtypeStruct((D, tokens), jnp.bfloat16),
        ),
        in_specs=[SMEM, HBM, HBM],
        out_specs=(VMEM, VMEM),
        scratch_shapes=[
            pltpu.VMEM((tokens, len(picks) * ROWS), jnp.bfloat16),
            pltpu.SemaphoreType.DMA((len(picks),)),
            pltpu.VMEM(upstream.shape, upstream.dtype),
            pltpu.SemaphoreType.DMA,
        ],
        compiler_params=pltpu.CompilerParams(vmem_limit_bytes=16 * 2**20),
        cost_estimate=LONG,
        name="first_terms",
    )(blocks, in_hbm(upstream), in_hbm(preactivation))


def terms_body(picks, parts, adds, blocks, up_ref, pre_ref, *refs):
    ins, outs = refs[: sum(map(len, adds))], refs[sum(map(len, adds)) :]
    zero = jnp.zeros((), jnp.bfloat16)
    picks = list(picks)
    for part, offsets, out in zip(parts, adds, outs):
        mine, ins = ins[: len(offsets)], ins[len(offsets) :]
        for k in range(part):
            start = pl.multiple_of(blocks[picks.pop(0)] * ROWS, ROWS)
            total = jnp.dot(
                up_ref[...],
                jnp.maximum(pre_ref[:, pl.ds(start, ROWS)], zero),
                preferred_element_type=jnp.float32,
            )
            for ref, offset in zip(mine, offsets):
                begin = offset + k * D
                total = total + ref[begin : begin + D, :].astype(jnp.float32)
            out[k * D : (k + 1) * D, :] = total.astype(jnp.bfloat16)


def terms(preactivation, up_t, blocks, picks, parts, adds=None, cost=SHORT):
    adds = adds or [()] * len(parts)
    offsets = [[begin for _, begin in group] for group in adds]

    def body(*refs):
        terms_body(picks, parts, offsets, *refs)

    return pl.pallas_call(
        body,
        out_shape=tuple(jax.ShapeDtypeStruct((p * D, ROWS), jnp.bfloat16) for p in parts),
        in_specs=[SMEM, VMEM, VMEM] + [VMEM] * sum(map(len, adds)),
        out_specs=tuple(VMEM for _ in parts),
        compiler_params=pltpu.CompilerParams(vmem_limit_bytes=16 * 2**20),
        cost_estimate=cost,
        name="terms",
    )(blocks, up_t, in_vmem(preactivation), *(a for group in adds for a, _ in group))


WIDE = 2048


def back_body(lo, up_ref, pre_ref, weight_ref, *refs):
    here = pl.ds(pl.multiple_of((pl.program_id(0) + lo) * WIDE, WIDE), WIDE)
    back = lax.dot_general(
        up_ref[...], weight_ref[here, :], (((1,), (1,)), ((), ())), preferred_element_type=jnp.float32
    )
    refs[-1][...] = jnp.where(
        pre_ref[:, here] > 0, back.astype(jnp.bfloat16), jnp.zeros((), jnp.bfloat16)
    )


def back_columns(lo, count, upstream, preactivation, weight, before):
    extra = [] if before is None else [before]
    tokens = preactivation.shape[0]

    def body(*refs):
        back_body(lo, *refs)

    return pl.pallas_call(
        body,
        out_shape=jax.ShapeDtypeStruct(preactivation.shape, jnp.bfloat16),
        grid=(count,),
        in_specs=[VMEM, VMEM, VMEM]
        + [pl.BlockSpec(memory_space=pl.ANY)] * len(extra),
        out_specs=pl.BlockSpec((tokens, WIDE), lambda i: (0, i + lo)),
        input_output_aliases={3: 0} if extra else {},
        compiler_params=pltpu.CompilerParams(vmem_limit_bytes=24 * 2**20),
        cost_estimate=LONG,
        name="back_columns",
    )(upstream, in_vmem(preactivation), in_vmem(weight), *map(in_hbm, extra))


def update_body(
    block, g0, g1, g2, g3, g4, g5, first, second, weight,
    first_out, second_out, update_out, short_out,
):
    beta_one = 0.9
    beta_two = 0.999
    bias_one = 1.0 - beta_one**STEP
    bias_two = 1.0 - beta_two**STEP
    start = pl.multiple_of(block[0] * ROWS, ROWS)
    own = pl.ds(start, ROWS)
    update_sq = jnp.zeros((8, 128), jnp.float32)
    weight_sq = jnp.zeros((8, 128), jnp.float32)
    for j in range(D // 128):
        part = slice(j * 128, (j + 1) * 128)
        total = g0[part, :].astype(jnp.float32)
        for ref in (g1, g2, g3, g4, g5):
            total = total + ref[part, :].astype(jnp.float32)
        gradient = total.T
        first_next = beta_one * first[:, part] + (1.0 - beta_one) * gradient
        second_next = beta_two * second[:, part] + (1.0 - beta_two) * gradient * gradient
        own_weight = weight[own, part].astype(jnp.float32)
        update = (
            first_next * (1.0 / bias_one) / (jnp.sqrt(second_next * (1.0 / bias_two)) + 1e-06)
            + 0.02 * own_weight
        )
        first_out[:, part] = first_next
        second_out[:, part] = second_next
        update_out[:, part] = update
        short_out[0:ROWS, part] = update.astype(jnp.bfloat16)
        update_sq = update_sq + jnp.sum((update * update).reshape(ROWS // 8, 8, 128), axis=0)
        weight_sq = weight_sq + jnp.sum(
            (own_weight * own_weight).reshape(ROWS // 8, 8, 128), axis=0
        )
    for k, norm in enumerate((update_sq, weight_sq)):
        lines = slice(ROWS + 8 * k, ROWS + 8 * k + 8)
        for j in range(3):
            piece = norm.astype(jnp.bfloat16)
            short_out[lines, j * 128 : (j + 1) * 128] = piece
            norm = norm - piece.astype(jnp.float32)
        short_out[lines, 384:512] = jnp.zeros((8, 128), jnp.bfloat16)


def update_rows(block, parts, first, second, weight):
    long = jax.ShapeDtypeStruct((ROWS, D), jnp.float32)
    return pl.pallas_call(
        update_body,
        out_shape=(
            long,
            long,
            long,
            jax.ShapeDtypeStruct((ROWS + 16, D), jnp.bfloat16),
        ),
        in_specs=[SMEM] + [VMEM] * 9,
        out_specs=(VMEM,) * 4,
        compiler_params=pltpu.CompilerParams(vmem_limit_bytes=16 * 2**20),
        cost_estimate=SHORT,
        name="update_rows",
    )(block, *parts, first, second, in_vmem(weight))


def apply_body(picks, sizes, trust, blocks, sums_ref, weight, *refs):
    updates = refs[: len(sizes)]
    ready, stored = refs[-2:]
    if trust:
        update_ref, out, trust_out = refs[len(sizes)], refs[-4], refs[-3]
    else:
        out = refs[-3]
    update_sq = jnp.sum(sums_ref[0:8, :], axis=(0, 1), keepdims=True)
    weight_sq = jnp.sum(sums_ref[8:16, :], axis=(0, 1), keepdims=True)
    ratio = jnp.sqrt(weight_sq) / jnp.sqrt(update_sq)
    step = (0.02 * ratio).astype(jnp.bfloat16)
    places = [(update, k) for size, update in zip(sizes, updates) for k in range(size)]
    stores = []
    for i, (update, k) in enumerate(places):
        begin = pl.multiple_of(blocks[picks[i]] * ROWS, ROWS)
        ready[i] = weight[pl.ds(begin, ROWS), :] - step * update[k * ROWS : (k + 1) * ROWS, :]
        stores.append(
            pltpu.make_async_copy(ready.at[i], out.at[pl.ds(begin, ROWS)], stored.at[i])
        )
        stores[-1].start()
    if trust:
        trust_out[...] = ratio * update_ref[...]
    for store in stores:
        store.wait()


def apply_update(blocks, picks, sums, weight, updates, update, before):
    sizes = [u.shape[0] // ROWS for u in updates]
    count = sum(sizes)
    trust = [] if update is None else [update]
    extra = [] if before is None else [before]

    def body(*refs):
        apply_body(picks, sizes, bool(trust), *refs)

    return pl.pallas_call(
        body,
        out_shape=(jax.ShapeDtypeStruct(weight.shape, jnp.bfloat16),)
        + tuple(jax.ShapeDtypeStruct(u.shape, u.dtype) for u in trust),
        in_specs=[SMEM, VMEM, VMEM] + [VMEM] * (len(updates) + len(trust)) + [HBM] * len(extra),
        out_specs=(HBM,) + (VMEM,) * len(trust),
        input_output_aliases={3 + len(updates) + len(trust): 0} if extra else {},
        scratch_shapes=[
            pltpu.VMEM((count, ROWS, D), jnp.bfloat16),
            pltpu.SemaphoreType.DMA((count,)),
        ],
        compiler_params=pltpu.CompilerParams(vmem_limit_bytes=16 * 2**20),
        cost_estimate=SHORT,
        name="apply_update",
    )(blocks, sums, in_vmem(weight), *updates, *trust, *map(in_hbm, extra))


def joined(*values):
    def body(*refs):
        rows_out, sums_out = refs[-2:]
        total = jnp.zeros((16, 128), jnp.float32)
        for k, ref in enumerate(refs[:-2]):
            rows_out[k * ROWS : (k + 1) * ROWS, :] = ref[0:ROWS, :]
            for j in range(3):
                total = total + ref[ROWS : ROWS + 16, j * 128 : (j + 1) * 128].astype(jnp.float32)
        sums_out[...] = total

    return pl.pallas_call(
        body,
        out_shape=(
            jax.ShapeDtypeStruct((len(values) * ROWS, D), jnp.bfloat16),
            jax.ShapeDtypeStruct((16, 128), jnp.float32),
        ),
        in_specs=[VMEM] * len(values),
        out_specs=(VMEM, VMEM),
        compiler_params=pltpu.CompilerParams(vmem_limit_bytes=16 * 2**20),
        cost_estimate=SHORT,
        name="joined",
    )(*values)


def taken(value, begin):
    rows = value.shape[0] // 2

    def body(ref, out):
        out[...] = ref[begin : begin + rows, :]

    return pl.pallas_call(
        body,
        out_shape=jax.ShapeDtypeStruct((rows, value.shape[1]), value.dtype),
        in_specs=[VMEM],
        out_specs=VMEM,
        compiler_params=pltpu.CompilerParams(vmem_limit_bytes=16 * 2**20),
        cost_estimate=SHORT,
        name="taken",
    )(value)


def added(*values):
    total = values[0].astype(jnp.float32)
    for value in values[1:]:
        total = total + value.astype(jnp.float32)
    return total.astype(jnp.bfloat16)


def own_unit(k):
    return [k * 4 + j for j in range(4)]


def other_unit(k):
    return [16 + k * 4 + j for j in range(4)]


def per_device(preactivation, upstream, weight, first_moment, second_moment):
    x, z, c = lax.axis_index("x"), lax.axis_index("z"), lax.axis_index("c")
    first = jnp.where(c == 0, x, z)
    second = jnp.where(c == 0, z, x)
    first_stride = jnp.where(c == 0, 8, 2)
    second_stride = jnp.where(c == 0, 2, 8)
    place = jnp.arange(32, dtype=jnp.int32)
    unit, member = (place >> 2) & 3, place & 3
    mine = place < 16
    on_first = first ^ jnp.where(mine, unit, member)
    on_second = second ^ jnp.where(mine, member, unit)
    blocks = on_first * first_stride + on_second * second_stride + jnp.where(mine, c, 1 - c)

    near_free = lambda unit: unit(1)[:2] + unit(3)[2:]
    near_late = lambda unit: unit(1)[2:] + unit(3)[:2]

    send_far, up_t = first_terms(preactivation, upstream, blocks, other_unit(2))

    def part(picks, parts, adds=None, then=(), cost=SHORT):
        return terms(preactivation, after(up_t, *then), blocks, picks, parts, adds, cost)

    got_far = sibling(send_far)
    keep_far = part(own_unit(2), (2, 2), then=(send_far,), cost=LONG)
    half = 2 * D
    (send_free,) = part(near_free(other_unit), (4,), then=keep_far)
    keep_far = [after(v, send_free) for v in keep_far]
    far_low = added(keep_far[0], got_far[:half])
    far_high = added(keep_far[1], got_far[half:])
    from_one = along_first(far_low, 1)
    from_three = along_first(far_high, 3)

    got_free = sibling(send_free)
    (send_late,) = part(near_late(other_unit), (4,), then=(far_low, far_high), cost=LONG)
    got_late = sibling(send_late)
    one_low, three_high = part(
        near_free(own_unit), (2, 2), [[(got_free, 0)], [(got_free, half)]], then=(send_late,)
    )
    sum_one_low = along_first(one_low, 1)
    sum_three_high = along_first(three_high, 3)
    (send_here,) = part(other_unit(0), (4,), then=(one_low, three_high), cost=LONG)
    got_here = sibling(send_here)
    one_high, three_low = part(
        near_late(own_unit),
        (2, 2),
        [[(got_late, 0), (from_three, 0)], [(got_late, half), (from_one, 0)]],
        then=(send_here,),
    )
    sum_one_high = along_first(one_high, 1)
    sum_three_low = along_first(three_low, 3)
    input_grad = back_columns(
        0, 2, after(upstream, one_high, three_low), preactivation, weight, None
    )
    (here,) = part(own_unit(0), (4,), [[(got_here, 0)]], then=(input_grad,))
    near = (
        added(here[D:half], sum_one_low[D:], sum_three_low[D:]),
        added(here[half : half + D], sum_one_high[:D], sum_three_high[:D]),
        added(here[half + D :], sum_one_high[D:], sum_three_high[D:]),
    )
    got = [along_second(v, k) for v, k in zip(near, (1, 2, 3))]
    input_grad = back_columns(2, 2, after(upstream, *near), preactivation, weight, input_grad)
    first_next, second_next, update, short = update_rows(
        blocks,
        [here, sum_one_low, sum_three_low, *got],
        first_moment,
        second_moment,
        after(weight, input_grad),
    )

    mine, sums = joined(short, *(along_second(short, k) for k in (1, 2, 3)))
    near_one = along_first(mine, 1)
    near_three = along_first(mine, 3)
    sums = sums + along_y(sums, 1)
    sums = sums + along_y(sums, 3)
    sums = sums + along_first(sums, 1) + along_first(sums, 2) + along_first(sums, 3)
    low = taken(after(near_one, sums), 0)
    high = taken(after(near_three, sums), 2 * ROWS)
    far_low = along_first(low, 3)
    far_high = along_first(high, 1)
    sums = after(sums, low, high)
    near_one, near_three = after(near_one, low, high), after(near_three, low, high)
    others = [sibling(v) for v in (after(mine, low, high), near_one, near_three)]
    sums = sums + sibling(sums)
    new_weight, trust_step = apply_update(
        blocks,
        own_unit(0) + own_unit(1) + own_unit(3) + own_unit(2),
        sums,
        weight,
        [mine, near_one, near_three, far_low, far_high],
        update,
        None,
    )
    (new_weight,) = apply_update(
        blocks,
        other_unit(0) + other_unit(1) + other_unit(3) + other_unit(2),
        sums,
        weight,
        [*others, sibling(far_low), sibling(far_high)],
        None,
        new_weight,
    )
    return (input_grad, new_weight, first_next, second_next, trust_step)


def solution(mesh):
    split = Mesh(mesh.devices.reshape(4, 4, 2, 4), ("x", "z", "c", "y"))
    rows = P(("y", "x", "z", "c"), None)
    return jax.shard_map(
        per_device,
        mesh=split,
        in_specs=(P(DP, "y"), P(DP, None), P("y", None), rows, rows),
        out_specs=(P(DP, "y"), P("y", None), rows, rows, rows),
        check_vma=False,
    )
```

```python
import jax
import jax.numpy as jnp
from jax import lax
from jax.experimental import pallas as pl
from jax.experimental.pallas import tpu as pltpu
from jax.sharding import Mesh
from jax.sharding import PartitionSpec as P

STEP = 1000
DP = ("x", "z", "c")
ROWS = 256
D = 512
VMEM = pl.BlockSpec(memory_space=pltpu.VMEM)
SMEM = pl.BlockSpec(memory_space=pltpu.SMEM)
HBM = pl.BlockSpec(memory_space=pltpu.HBM)
SHORT = pl.CostEstimate(flops=2**20, bytes_accessed=2**16, transcendentals=0)
LONG = pl.CostEstimate(flops=2**34, bytes_accessed=2**26, transcendentals=0)


def exchanges(axis, k):
    pairs = []
    for x in range(4):
        for z in range(4):
            for c in range(2):
                along_x = (axis == "first") == (c == 0)
                to_x, to_z = (x ^ k, z) if along_x else (x, z ^ k)
                pairs.append(((x * 4 + z) * 2 + c, (to_x * 4 + to_z) * 2 + c))
    return pairs


def along_first(value, k):
    return lax.ppermute(value, DP, exchanges("first", k))


def along_second(value, k):
    return lax.ppermute(value, DP, exchanges("second", k))


def along_y(value, k):
    return lax.ppermute(value, "y", [(y, y ^ k) for y in range(4)])


def sibling(value):
    return lax.ppermute(value, "c", [(0, 1), (1, 0)])


def in_hbm(value):
    return pltpu.with_memory_space_constraint(value, pltpu.HBM)


def in_vmem(value):
    return pltpu.with_memory_space_constraint(value, pltpu.VMEM)


def after(value, *others):
    return lax.optimization_barrier((value, *others))[0]


def first_body(picks, blocks, up_ref, pre_ref, out, up_t, columns, arrived, up, up_arrived):
    copies = []
    up_copy = pltpu.make_async_copy(up_ref, up, up_arrived)
    up_copy.start()
    for i, pick in enumerate(picks):
        start = pl.multiple_of(blocks[pick] * ROWS, ROWS)
        copies.append(
            pltpu.make_async_copy(
                pre_ref.at[:, pl.ds(start, ROWS)],
                columns.at[:, pl.ds(i * ROWS, ROWS)],
                arrived.at[i],
            )
        )
        copies[-1].start()
    up_copy.wait()
    up_t[...] = up[...].T
    zero = jnp.zeros((), jnp.bfloat16)
    for i, copy in enumerate(copies):
        copy.wait()
        out[i * D : (i + 1) * D, :] = jnp.dot(
            up_t[...],
            jnp.maximum(columns[:, i * ROWS : (i + 1) * ROWS], zero),
            preferred_element_type=jnp.float32,
        ).astype(jnp.bfloat16)


def first_terms(preactivation, upstream, blocks, picks):
    tokens = preactivation.shape[0]

    def body(*refs):
        first_body(picks, *refs)

    return pl.pallas_call(
        body,
        out_shape=(
            jax.ShapeDtypeStruct((len(picks) * D, ROWS), jnp.bfloat16),
            jax.ShapeDtypeStruct((D, tokens), jnp.bfloat16),
        ),
        in_specs=[SMEM, HBM, HBM],
        out_specs=(VMEM, VMEM),
        scratch_shapes=[
            pltpu.VMEM((tokens, len(picks) * ROWS), jnp.bfloat16),
            pltpu.SemaphoreType.DMA((len(picks),)),
            pltpu.VMEM(upstream.shape, upstream.dtype),
            pltpu.SemaphoreType.DMA,
        ],
        compiler_params=pltpu.CompilerParams(vmem_limit_bytes=16 * 2**20),
        cost_estimate=LONG,
        name="first_terms",
    )(blocks, in_hbm(upstream), in_hbm(preactivation))


def terms_body(picks, parts, adds, blocks, up_ref, pre_ref, *refs):
    ins, outs = refs[: sum(map(len, adds))], refs[sum(map(len, adds)) :]
    zero = jnp.zeros((), jnp.bfloat16)
    picks = list(picks)
    for part, offsets, out in zip(parts, adds, outs):
        mine, ins = ins[: len(offsets)], ins[len(offsets) :]
        for k in range(part):
            start = pl.multiple_of(blocks[picks.pop(0)] * ROWS, ROWS)
            total = jnp.dot(
                up_ref[...],
                jnp.maximum(pre_ref[:, pl.ds(start, ROWS)], zero),
                preferred_element_type=jnp.float32,
            )
            for ref, offset in zip(mine, offsets):
                begin = offset + k * D
                total = total + ref[begin : begin + D, :].astype(jnp.float32)
            out[k * D : (k + 1) * D, :] = total.astype(jnp.bfloat16)


def terms(preactivation, up_t, blocks, picks, parts, adds=None, cost=SHORT):
    adds = adds or [()] * len(parts)
    offsets = [[begin for _, begin in group] for group in adds]

    def body(*refs):
        terms_body(picks, parts, offsets, *refs)

    return pl.pallas_call(
        body,
        out_shape=tuple(jax.ShapeDtypeStruct((p * D, ROWS), jnp.bfloat16) for p in parts),
        in_specs=[SMEM, VMEM, VMEM] + [VMEM] * sum(map(len, adds)),
        out_specs=tuple(VMEM for _ in parts),
        compiler_params=pltpu.CompilerParams(vmem_limit_bytes=16 * 2**20),
        cost_estimate=cost,
        name="terms",
    )(blocks, up_t, in_vmem(preactivation), *(a for group in adds for a, _ in group))


WIDE = 2048


def back_body(lo, up_ref, pre_ref, weight_ref, *refs):
    here = pl.ds(pl.multiple_of((pl.program_id(0) + lo) * WIDE, WIDE), WIDE)
    back = lax.dot_general(
        up_ref[...], weight_ref[here, :], (((1,), (1,)), ((), ())), preferred_element_type=jnp.float32
    )
    refs[-1][...] = jnp.where(
        pre_ref[:, here] > 0, back.astype(jnp.bfloat16), jnp.zeros((), jnp.bfloat16)
    )


def back_columns(lo, count, upstream, preactivation, weight, before):
    extra = [] if before is None else [before]
    tokens = preactivation.shape[0]

    def body(*refs):
        back_body(lo, *refs)

    return pl.pallas_call(
        body,
        out_shape=jax.ShapeDtypeStruct(preactivation.shape, jnp.bfloat16),
        grid=(count,),
        in_specs=[VMEM, VMEM, VMEM]
        + [pl.BlockSpec(memory_space=pl.ANY)] * len(extra),
        out_specs=pl.BlockSpec((tokens, WIDE), lambda i: (0, i + lo)),
        input_output_aliases={3: 0} if extra else {},
        compiler_params=pltpu.CompilerParams(vmem_limit_bytes=24 * 2**20),
        cost_estimate=LONG,
        name="back_columns",
    )(upstream, in_vmem(preactivation), in_vmem(weight), *map(in_hbm, extra))


def update_body(
    block, g0, g1, g2, g3, g4, g5, first, second, weight,
    first_out, second_out, update_out, short_out,
):
    beta_one = 0.9
    beta_two = 0.999
    bias_one = 1.0 - beta_one**STEP
    bias_two = 1.0 - beta_two**STEP
    start = pl.multiple_of(block[0] * ROWS, ROWS)
    own = pl.ds(start, ROWS)
    update_sq = jnp.zeros((8, 128), jnp.float32)
    weight_sq = jnp.zeros((8, 128), jnp.float32)
    for j in range(D // 128):
        part = slice(j * 128, (j + 1) * 128)
        total = g0[part, :].astype(jnp.float32)
        for ref in (g1, g2, g3, g4, g5):
            total = total + ref[part, :].astype(jnp.float32)
        gradient = total.T
        first_next = beta_one * first[:, part] + (1.0 - beta_one) * gradient
        second_next = beta_two * second[:, part] + (1.0 - beta_two) * gradient * gradient
        own_weight = weight[own, part].astype(jnp.float32)
        update = (
            first_next * (1.0 / bias_one) / (jnp.sqrt(second_next * (1.0 / bias_two)) + 1e-06)
            + 0.02 * own_weight
        )
        first_out[:, part] = first_next
        second_out[:, part] = second_next
        update_out[:, part] = update
        short_out[0:ROWS, part] = update.astype(jnp.bfloat16)
        update_sq = update_sq + jnp.sum((update * update).reshape(ROWS // 8, 8, 128), axis=0)
        weight_sq = weight_sq + jnp.sum(
            (own_weight * own_weight).reshape(ROWS // 8, 8, 128), axis=0
        )
    for k, norm in enumerate((update_sq, weight_sq)):
        lines = slice(ROWS + 8 * k, ROWS + 8 * k + 8)
        for j in range(3):
            piece = norm.astype(jnp.bfloat16)
            short_out[lines, j * 128 : (j + 1) * 128] = piece
            norm = norm - piece.astype(jnp.float32)
        short_out[lines, 384:512] = jnp.zeros((8, 128), jnp.bfloat16)


def update_rows(block, parts, first, second, weight):
    long = jax.ShapeDtypeStruct((ROWS, D), jnp.float32)
    return pl.pallas_call(
        update_body,
        out_shape=(
            long,
            long,
            long,
            jax.ShapeDtypeStruct((ROWS + 16, D), jnp.bfloat16),
        ),
        in_specs=[SMEM] + [VMEM] * 9,
        out_specs=(VMEM,) * 4,
        compiler_params=pltpu.CompilerParams(vmem_limit_bytes=16 * 2**20),
        cost_estimate=SHORT,
        name="update_rows",
    )(block, *parts, first, second, in_vmem(weight))


def apply_body(picks, sizes, trust, blocks, sums_ref, weight, *refs):
    updates = refs[: len(sizes)]
    ready, stored = refs[-2:]
    if trust:
        update_ref, out, trust_out = refs[len(sizes)], refs[-4], refs[-3]
    else:
        out = refs[-3]
    update_sq = jnp.sum(sums_ref[0:8, :], axis=(0, 1), keepdims=True)
    weight_sq = jnp.sum(sums_ref[8:16, :], axis=(0, 1), keepdims=True)
    ratio = jnp.sqrt(weight_sq) / jnp.sqrt(update_sq)
    step = (0.02 * ratio).astype(jnp.bfloat16)
    places = [(update, k) for size, update in zip(sizes, updates) for k in range(size)]
    stores = []
    for i, (update, k) in enumerate(places):
        begin = pl.multiple_of(blocks[picks[i]] * ROWS, ROWS)
        ready[i] = weight[pl.ds(begin, ROWS), :] - step * update[k * ROWS : (k + 1) * ROWS, :]
        stores.append(
            pltpu.make_async_copy(ready.at[i], out.at[pl.ds(begin, ROWS)], stored.at[i])
        )
        stores[-1].start()
    if trust:
        trust_out[...] = ratio * update_ref[...]
    for store in stores:
        store.wait()


def apply_update(blocks, picks, sums, weight, updates, update, before):
    sizes = [u.shape[0] // ROWS for u in updates]
    count = sum(sizes)
    trust = [] if update is None else [update]
    extra = [] if before is None else [before]

    def body(*refs):
        apply_body(picks, sizes, bool(trust), *refs)

    return pl.pallas_call(
        body,
        out_shape=(jax.ShapeDtypeStruct(weight.shape, jnp.bfloat16),)
        + tuple(jax.ShapeDtypeStruct(u.shape, u.dtype) for u in trust),
        in_specs=[SMEM, VMEM, VMEM] + [VMEM] * (len(updates) + len(trust)) + [HBM] * len(extra),
        out_specs=(HBM,) + (VMEM,) * len(trust),
        input_output_aliases={3 + len(updates) + len(trust): 0} if extra else {},
        scratch_shapes=[
            pltpu.VMEM((count, ROWS, D), jnp.bfloat16),
            pltpu.SemaphoreType.DMA((count,)),
        ],
        compiler_params=pltpu.CompilerParams(vmem_limit_bytes=16 * 2**20),
        cost_estimate=SHORT,
        name="apply_update",
    )(blocks, sums, in_vmem(weight), *updates, *trust, *map(in_hbm, extra))


def joined(*values):
    def body(*refs):
        rows_out, sums_out = refs[-2:]
        total = jnp.zeros((16, 128), jnp.float32)
        for k, ref in enumerate(refs[:-2]):
            rows_out[k * ROWS : (k + 1) * ROWS, :] = ref[0:ROWS, :]
            for j in range(3):
                total = total + ref[ROWS : ROWS + 16, j * 128 : (j + 1) * 128].astype(jnp.float32)
        sums_out[...] = total

    return pl.pallas_call(
        body,
        out_shape=(
            jax.ShapeDtypeStruct((len(values) * ROWS, D), jnp.bfloat16),
            jax.ShapeDtypeStruct((16, 128), jnp.float32),
        ),
        in_specs=[VMEM] * len(values),
        out_specs=(VMEM, VMEM),
        compiler_params=pltpu.CompilerParams(vmem_limit_bytes=16 * 2**20),
        cost_estimate=SHORT,
        name="joined",
    )(*values)


def taken(value, begin):
    rows = value.shape[0] // 2

    def body(ref, out):
        out[...] = ref[begin : begin + rows, :]

    return pl.pallas_call(
        body,
        out_shape=jax.ShapeDtypeStruct((rows, value.shape[1]), value.dtype),
        in_specs=[VMEM],
        out_specs=VMEM,
        compiler_params=pltpu.CompilerParams(vmem_limit_bytes=16 * 2**20),
        cost_estimate=SHORT,
        name="taken",
    )(value)


def added(*values):
    total = values[0].astype(jnp.float32)
    for value in values[1:]:
        total = total + value.astype(jnp.float32)
    return total.astype(jnp.bfloat16)


def own_unit(k):
    return [k * 4 + j for j in range(4)]


def other_unit(k):
    return [16 + k * 4 + j for j in range(4)]


def per_device(preactivation, upstream, weight, first_moment, second_moment):
    x, z, c = lax.axis_index("x"), lax.axis_index("z"), lax.axis_index("c")
    first = jnp.where(c == 0, x, z)
    second = jnp.where(c == 0, z, x)
    first_stride = jnp.where(c == 0, 8, 2)
    second_stride = jnp.where(c == 0, 2, 8)
    place = jnp.arange(32, dtype=jnp.int32)
    unit, member = (place >> 2) & 3, place & 3
    mine = place < 16
    on_first = first ^ jnp.where(mine, unit, member)
    on_second = second ^ jnp.where(mine, member, unit)
    blocks = on_first * first_stride + on_second * second_stride + jnp.where(mine, c, 1 - c)

    near_free = lambda unit: unit(1)[:2] + unit(3)[2:]
    near_late = lambda unit: unit(1)[2:] + unit(3)[:2]

    send_far, up_t = first_terms(preactivation, upstream, blocks, other_unit(2))

    def part(picks, parts, adds=None, then=(), cost=SHORT):
        return terms(preactivation, after(up_t, *then), blocks, picks, parts, adds, cost)

    got_far = sibling(send_far)
    keep_far = part(own_unit(2), (2, 2), then=(send_far,), cost=LONG)
    half = 2 * D
    (send_free,) = part(near_free(other_unit), (4,), then=keep_far)
    keep_far = [after(v, send_free) for v in keep_far]
    far_low = added(keep_far[0], got_far[:half])
    far_high = added(keep_far[1], got_far[half:])
    from_one = along_first(far_low, 1)
    from_three = along_first(far_high, 3)

    got_free = sibling(send_free)
    (send_late,) = part(near_late(other_unit), (4,), then=(far_low, far_high), cost=LONG)
    got_late = sibling(send_late)
    one_low, three_high = part(
        near_free(own_unit), (2, 2), [[(got_free, 0)], [(got_free, half)]], then=(send_late,)
    )
    sum_one_low = along_first(one_low, 1)
    sum_three_high = along_first(three_high, 3)
    (send_here,) = part(other_unit(0), (4,), then=(one_low, three_high), cost=LONG)
    got_here = sibling(send_here)
    one_high, three_low = part(
        near_late(own_unit),
        (2, 2),
        [[(got_late, 0), (from_three, 0)], [(got_late, half), (from_one, 0)]],
        then=(send_here,),
    )
    sum_one_high = along_first(one_high, 1)
    sum_three_low = along_first(three_low, 3)
    input_grad = back_columns(
        0, 2, after(upstream, one_high, three_low), preactivation, weight, None
    )
    (here,) = part(own_unit(0), (4,), [[(got_here, 0)]], then=(input_grad,))
    near = (
        added(here[D:half], sum_one_low[D:], sum_three_low[D:]),
        added(here[half : half + D], sum_one_high[:D], sum_three_high[:D]),
        added(here[half + D :], sum_one_high[D:], sum_three_high[D:]),
    )
    got = [along_second(v, k) for v, k in zip(near, (1, 2, 3))]
    input_grad = back_columns(2, 2, after(upstream, *near), preactivation, weight, input_grad)
    first_next, second_next, update, short = update_rows(
        blocks,
        [here, sum_one_low, sum_three_low, *got],
        first_moment,
        second_moment,
        after(weight, input_grad),
    )

    mine, sums = joined(short, *(along_second(short, k) for k in (1, 2, 3)))
    near_one = along_first(mine, 1)
    near_three = along_first(mine, 3)
    sums = sums + along_y(sums, 1)
    sums = sums + along_y(sums, 3)
    sums = sums + along_first(sums, 1) + along_first(sums, 2) + along_first(sums, 3)
    low = taken(after(near_one, sums), 0)
    high = taken(after(near_three, sums), 2 * ROWS)
    far_low = along_first(low, 3)
    far_high = along_first(high, 1)
    sums = after(sums, low, high)
    near_one, near_three = after(near_one, low, high), after(near_three, low, high)
    others = [sibling(v) for v in (after(mine, low, high), near_one, near_three)]
    sums = sums + sibling(after(sums, others[0]))
    new_weight, trust_step = apply_update(
        blocks,
        own_unit(0) + own_unit(1) + own_unit(3) + other_unit(0) + other_unit(1) + other_unit(3),
        sums,
        weight,
        [mine, near_one, near_three, *others],
        update,
        None,
    )
    far_low, far_high = after(far_low, new_weight), after(far_high, new_weight)
    (new_weight,) = apply_update(
        blocks,
        own_unit(2) + other_unit(2),
        sums,
        weight,
        [far_low, far_high, sibling(far_low), sibling(far_high)],
        None,
        new_weight,
    )
    return (input_grad, new_weight, first_next, second_next, trust_step)


def solution(mesh):
    split = Mesh(mesh.devices.reshape(4, 4, 2, 4), ("x", "z", "c", "y"))
    rows = P(("y", "x", "z", "c"), None)
    return jax.shard_map(
        per_device,
        mesh=split,
        in_specs=(P(DP, "y"), P(DP, None), P("y", None), rows, rows),
        out_specs=(P(DP, "y"), P("y", None), rows, rows, rows),
        check_vma=False,
    )
```

```python
import jax
import jax.numpy as jnp
from jax import lax
from jax.experimental import pallas as pl
from jax.experimental.pallas import tpu as pltpu
from jax.sharding import Mesh
from jax.sharding import PartitionSpec as P

STEP = 1000
DP = ("x", "z", "c")
ROWS = 256
D = 512
VMEM = pl.BlockSpec(memory_space=pltpu.VMEM)
SMEM = pl.BlockSpec(memory_space=pltpu.SMEM)
HBM = pl.BlockSpec(memory_space=pltpu.HBM)
SHORT = pl.CostEstimate(flops=2**20, bytes_accessed=2**16, transcendentals=0)
LONG = pl.CostEstimate(flops=2**34, bytes_accessed=2**26, transcendentals=0)


def exchanges(axis, k):
    pairs = []
    for x in range(4):
        for z in range(4):
            for c in range(2):
                along_x = (axis == "first") == (c == 0)
                to_x, to_z = (x ^ k, z) if along_x else (x, z ^ k)
                pairs.append(((x * 4 + z) * 2 + c, (to_x * 4 + to_z) * 2 + c))
    return pairs


def along_first(value, k):
    return lax.ppermute(value, DP, exchanges("first", k))


def along_second(value, k):
    return lax.ppermute(value, DP, exchanges("second", k))


def along_y(value, k):
    return lax.ppermute(value, "y", [(y, y ^ k) for y in range(4)])


def sibling(value):
    return lax.ppermute(value, "c", [(0, 1), (1, 0)])


def in_hbm(value):
    return pltpu.with_memory_space_constraint(value, pltpu.HBM)


def in_vmem(value):
    return pltpu.with_memory_space_constraint(value, pltpu.VMEM)


def after(value, *others):
    return lax.optimization_barrier((value, *others))[0]


def first_body(picks, blocks, up_ref, pre_ref, out, up_t, columns, arrived, up, up_arrived):
    copies = []
    up_copy = pltpu.make_async_copy(up_ref, up, up_arrived)
    up_copy.start()
    for i, pick in enumerate(picks):
        start = pl.multiple_of(blocks[pick] * ROWS, ROWS)
        copies.append(
            pltpu.make_async_copy(
                pre_ref.at[:, pl.ds(start, ROWS)],
                columns.at[:, pl.ds(i * ROWS, ROWS)],
                arrived.at[i],
            )
        )
        copies[-1].start()
    up_copy.wait()
    up_t[...] = up[...].T
    zero = jnp.zeros((), jnp.bfloat16)
    for i, copy in enumerate(copies):
        copy.wait()
        out[i * D : (i + 1) * D, :] = jnp.dot(
            up_t[...],
            jnp.maximum(columns[:, i * ROWS : (i + 1) * ROWS], zero),
            preferred_element_type=jnp.float32,
        ).astype(jnp.bfloat16)


def first_terms(preactivation, upstream, blocks, picks):
    tokens = preactivation.shape[0]

    def body(*refs):
        first_body(picks, *refs)

    return pl.pallas_call(
        body,
        out_shape=(
            jax.ShapeDtypeStruct((len(picks) * D, ROWS), jnp.bfloat16),
            jax.ShapeDtypeStruct((D, tokens), jnp.bfloat16),
        ),
        in_specs=[SMEM, HBM, HBM],
        out_specs=(VMEM, VMEM),
        scratch_shapes=[
            pltpu.VMEM((tokens, len(picks) * ROWS), jnp.bfloat16),
            pltpu.SemaphoreType.DMA((len(picks),)),
            pltpu.VMEM(upstream.shape, upstream.dtype),
            pltpu.SemaphoreType.DMA,
        ],
        compiler_params=pltpu.CompilerParams(vmem_limit_bytes=16 * 2**20),
        cost_estimate=LONG,
        name="first_terms",
    )(blocks, in_hbm(upstream), in_hbm(preactivation))


def terms_body(picks, parts, adds, blocks, up_ref, pre_ref, *refs):
    ins, outs = refs[: sum(map(len, adds))], refs[sum(map(len, adds)) :]
    zero = jnp.zeros((), jnp.bfloat16)
    picks = list(picks)
    for part, offsets, out in zip(parts, adds, outs):
        mine, ins = ins[: len(offsets)], ins[len(offsets) :]
        for k in range(part):
            start = pl.multiple_of(blocks[picks.pop(0)] * ROWS, ROWS)
            total = jnp.dot(
                up_ref[...],
                jnp.maximum(pre_ref[:, pl.ds(start, ROWS)], zero),
                preferred_element_type=jnp.float32,
            )
            for ref, offset in zip(mine, offsets):
                begin = offset + k * D
                total = total + ref[begin : begin + D, :].astype(jnp.float32)
            out[k * D : (k + 1) * D, :] = total.astype(jnp.bfloat16)


def terms(preactivation, up_t, blocks, picks, parts, adds=None, cost=SHORT):
    adds = adds or [()] * len(parts)
    offsets = [[begin for _, begin in group] for group in adds]

    def body(*refs):
        terms_body(picks, parts, offsets, *refs)

    return pl.pallas_call(
        body,
        out_shape=tuple(jax.ShapeDtypeStruct((p * D, ROWS), jnp.bfloat16) for p in parts),
        in_specs=[SMEM, VMEM, VMEM] + [VMEM] * sum(map(len, adds)),
        out_specs=tuple(VMEM for _ in parts),
        compiler_params=pltpu.CompilerParams(vmem_limit_bytes=16 * 2**20),
        cost_estimate=cost,
        name="terms",
    )(blocks, up_t, in_vmem(preactivation), *(a for group in adds for a, _ in group))


WIDE = 2048


def back_body(lo, up_ref, pre_ref, weight_ref, *refs):
    here = pl.ds(pl.multiple_of((pl.program_id(0) + lo) * WIDE, WIDE), WIDE)
    back = lax.dot_general(
        up_ref[...], weight_ref[here, :], (((1,), (1,)), ((), ())), preferred_element_type=jnp.float32
    )
    refs[-1][...] = jnp.where(
        pre_ref[:, here] > 0, back.astype(jnp.bfloat16), jnp.zeros((), jnp.bfloat16)
    )


def back_columns(lo, count, upstream, preactivation, weight, before):
    extra = [] if before is None else [before]
    tokens = preactivation.shape[0]

    def body(*refs):
        back_body(lo, *refs)

    return pl.pallas_call(
        body,
        out_shape=jax.ShapeDtypeStruct(preactivation.shape, jnp.bfloat16),
        grid=(count,),
        in_specs=[VMEM, VMEM, VMEM]
        + [pl.BlockSpec(memory_space=pl.ANY)] * len(extra),
        out_specs=pl.BlockSpec((tokens, WIDE), lambda i: (0, i + lo)),
        input_output_aliases={3: 0} if extra else {},
        compiler_params=pltpu.CompilerParams(vmem_limit_bytes=24 * 2**20),
        cost_estimate=LONG,
        name="back_columns",
    )(upstream, in_vmem(preactivation), in_vmem(weight), *map(in_hbm, extra))


def update_body(
    block, g0, g1, g2, g3, g4, g5, first, second, weight,
    first_out, second_out, update_out, short_out,
):
    beta_one = 0.9
    beta_two = 0.999
    bias_one = 1.0 - beta_one**STEP
    bias_two = 1.0 - beta_two**STEP
    start = pl.multiple_of(block[0] * ROWS, ROWS)
    own = pl.ds(start, ROWS)
    update_sq = jnp.zeros((8, 128), jnp.float32)
    weight_sq = jnp.zeros((8, 128), jnp.float32)
    for j in range(D // 128):
        part = slice(j * 128, (j + 1) * 128)
        total = g0[part, :].astype(jnp.float32)
        for ref in (g1, g2, g3, g4, g5):
            total = total + ref[part, :].astype(jnp.float32)
        gradient = total.T
        first_next = beta_one * first[:, part] + (1.0 - beta_one) * gradient
        second_next = beta_two * second[:, part] + (1.0 - beta_two) * gradient * gradient
        own_weight = weight[own, part].astype(jnp.float32)
        update = (
            first_next * (1.0 / bias_one) / (jnp.sqrt(second_next * (1.0 / bias_two)) + 1e-06)
            + 0.02 * own_weight
        )
        first_out[:, part] = first_next
        second_out[:, part] = second_next
        update_out[:, part] = update
        short_out[0:ROWS, part] = update.astype(jnp.bfloat16)
        update_sq = update_sq + jnp.sum((update * update).reshape(ROWS // 8, 8, 128), axis=0)
        weight_sq = weight_sq + jnp.sum(
            (own_weight * own_weight).reshape(ROWS // 8, 8, 128), axis=0
        )
    for k, norm in enumerate((update_sq, weight_sq)):
        lines = slice(ROWS + 8 * k, ROWS + 8 * k + 8)
        for j in range(3):
            piece = norm.astype(jnp.bfloat16)
            short_out[lines, j * 128 : (j + 1) * 128] = piece
            norm = norm - piece.astype(jnp.float32)
        short_out[lines, 384:512] = jnp.zeros((8, 128), jnp.bfloat16)


def update_rows(block, parts, first, second, weight):
    long = jax.ShapeDtypeStruct((ROWS, D), jnp.float32)
    return pl.pallas_call(
        update_body,
        out_shape=(
            long,
            long,
            long,
            jax.ShapeDtypeStruct((ROWS + 16, D), jnp.bfloat16),
        ),
        in_specs=[SMEM] + [VMEM] * 9,
        out_specs=(VMEM,) * 4,
        compiler_params=pltpu.CompilerParams(vmem_limit_bytes=16 * 2**20),
        cost_estimate=SHORT,
        name="update_rows",
    )(block, *parts, first, second, in_vmem(weight))


def apply_body(picks, sizes, trust, blocks, sums_ref, weight, *refs):
    updates = refs[: len(sizes)]
    ready, stored = refs[-2:]
    if trust:
        update_ref, out, trust_out = refs[len(sizes)], refs[-4], refs[-3]
    else:
        out = refs[-3]
    update_sq = jnp.sum(sums_ref[0:8, :], axis=(0, 1), keepdims=True)
    weight_sq = jnp.sum(sums_ref[8:16, :], axis=(0, 1), keepdims=True)
    ratio = jnp.sqrt(weight_sq) / jnp.sqrt(update_sq)
    step = (0.02 * ratio).astype(jnp.bfloat16)
    places = [(update, k) for size, update in zip(sizes, updates) for k in range(size)]
    stores = []
    for i, (update, k) in enumerate(places):
        begin = pl.multiple_of(blocks[picks[i]] * ROWS, ROWS)
        ready[i] = weight[pl.ds(begin, ROWS), :] - step * update[k * ROWS : (k + 1) * ROWS, :]
        stores.append(
            pltpu.make_async_copy(ready.at[i], out.at[pl.ds(begin, ROWS)], stored.at[i])
        )
        stores[-1].start()
    if trust:
        trust_out[...] = ratio * update_ref[...]
    for store in stores:
        store.wait()


def apply_update(blocks, picks, sums, weight, updates, update, before):
    sizes = [u.shape[0] // ROWS for u in updates]
    count = sum(sizes)
    trust = [] if update is None else [update]
    extra = [] if before is None else [before]

    def body(*refs):
        apply_body(picks, sizes, bool(trust), *refs)

    return pl.pallas_call(
        body,
        out_shape=(jax.ShapeDtypeStruct(weight.shape, jnp.bfloat16),)
        + tuple(jax.ShapeDtypeStruct(u.shape, u.dtype) for u in trust),
        in_specs=[SMEM, VMEM, VMEM] + [VMEM] * (len(updates) + len(trust)) + [HBM] * len(extra),
        out_specs=(HBM,) + (VMEM,) * len(trust),
        input_output_aliases={3 + len(updates) + len(trust): 0} if extra else {},
        scratch_shapes=[
            pltpu.VMEM((count, ROWS, D), jnp.bfloat16),
            pltpu.SemaphoreType.DMA((count,)),
        ],
        compiler_params=pltpu.CompilerParams(vmem_limit_bytes=16 * 2**20),
        cost_estimate=SHORT,
        name="apply_update",
    )(blocks, sums, in_vmem(weight), *updates, *trust, *map(in_hbm, extra))


def joined(*values):
    def body(*refs):
        rows_out, sums_out = refs[-2:]
        total = jnp.zeros((16, 128), jnp.float32)
        for k, ref in enumerate(refs[:-2]):
            rows_out[k * ROWS : (k + 1) * ROWS, :] = ref[0:ROWS, :]
            for j in range(3):
                total = total + ref[ROWS : ROWS + 16, j * 128 : (j + 1) * 128].astype(jnp.float32)
        sums_out[...] = total

    return pl.pallas_call(
        body,
        out_shape=(
            jax.ShapeDtypeStruct((len(values) * ROWS, D), jnp.bfloat16),
            jax.ShapeDtypeStruct((16, 128), jnp.float32),
        ),
        in_specs=[VMEM] * len(values),
        out_specs=(VMEM, VMEM),
        compiler_params=pltpu.CompilerParams(vmem_limit_bytes=16 * 2**20),
        cost_estimate=SHORT,
        name="joined",
    )(*values)


def taken(value, begin):
    rows = value.shape[0] // 2

    def body(ref, out):
        out[...] = ref[begin : begin + rows, :]

    return pl.pallas_call(
        body,
        out_shape=jax.ShapeDtypeStruct((rows, value.shape[1]), value.dtype),
        in_specs=[VMEM],
        out_specs=VMEM,
        compiler_params=pltpu.CompilerParams(vmem_limit_bytes=16 * 2**20),
        cost_estimate=SHORT,
        name="taken",
    )(value)


def added(*values):
    total = values[0].astype(jnp.float32)
    for value in values[1:]:
        total = total + value.astype(jnp.float32)
    return total.astype(jnp.bfloat16)


def own_unit(k):
    return [k * 4 + j for j in range(4)]


def other_unit(k):
    return [16 + k * 4 + j for j in range(4)]


def per_device(preactivation, upstream, weight, first_moment, second_moment):
    x, z, c = lax.axis_index("x"), lax.axis_index("z"), lax.axis_index("c")
    first = jnp.where(c == 0, x, z)
    second = jnp.where(c == 0, z, x)
    first_stride = jnp.where(c == 0, 8, 2)
    second_stride = jnp.where(c == 0, 2, 8)
    place = jnp.arange(32, dtype=jnp.int32)
    unit, member = (place >> 2) & 3, place & 3
    mine = place < 16
    on_first = first ^ jnp.where(mine, unit, member)
    on_second = second ^ jnp.where(mine, member, unit)
    blocks = on_first * first_stride + on_second * second_stride + jnp.where(mine, c, 1 - c)

    near_free = lambda unit: unit(1)[:2] + unit(3)[2:]
    near_late = lambda unit: unit(1)[2:] + unit(3)[:2]

    send_far, up_t = first_terms(preactivation, upstream, blocks, other_unit(2))

    def part(picks, parts, adds=None, then=(), cost=SHORT):
        return terms(preactivation, after(up_t, *then), blocks, picks, parts, adds, cost)

    got_far = sibling(send_far)
    keep_far = part(own_unit(2), (2, 2), then=(send_far,), cost=LONG)
    half = 2 * D
    (send_free,) = part(near_free(other_unit), (4,), then=keep_far)
    keep_far = [after(v, send_free) for v in keep_far]
    far_low = added(keep_far[0], got_far[:half])
    far_high = added(keep_far[1], got_far[half:])
    from_one = along_first(far_low, 1)
    from_three = along_first(far_high, 3)

    got_free = sibling(send_free)
    (send_late,) = part(near_late(other_unit), (4,), then=(far_low, far_high), cost=LONG)
    got_late = sibling(send_late)
    one_low, three_high = part(
        near_free(own_unit), (2, 2), [[(got_free, 0)], [(got_free, half)]], then=(send_late,)
    )
    sum_one_low = along_first(one_low, 1)
    sum_three_high = along_first(three_high, 3)
    (send_here,) = part(other_unit(0), (4,), then=(one_low, three_high), cost=LONG)
    got_here = sibling(send_here)
    one_high, three_low = part(
        near_late(own_unit),
        (2, 2),
        [[(got_late, 0), (from_three, 0)], [(got_late, half), (from_one, 0)]],
        then=(send_here,),
    )
    sum_one_high = along_first(one_high, 1)
    sum_three_low = along_first(three_low, 3)
    input_grad = back_columns(
        0, 2, after(upstream, one_high, three_low), preactivation, weight, None
    )
    (here,) = part(own_unit(0), (4,), [[(got_here, 0)]], then=(input_grad,))
    near = (
        added(here[D:half], sum_one_low[D:], sum_three_low[D:]),
        added(here[half : half + D], sum_one_high[:D], sum_three_high[:D]),
        added(here[half + D :], sum_one_high[D:], sum_three_high[D:]),
    )
    got = [along_second(v, k) for v, k in zip(near, (1, 2, 3))]
    input_grad = back_columns(2, 2, after(upstream, *near), preactivation, weight, input_grad)
    first_next, second_next, update, short = update_rows(
        blocks,
        [here, sum_one_low, sum_three_low, *got],
        first_moment,
        second_moment,
        after(weight, input_grad),
    )

    mine, sums = joined(short, *(along_second(short, k) for k in (1, 2, 3)))
    near_one = along_first(mine, 1)
    near_three = along_first(mine, 3)
    sums = sums + along_y(sums, 1)
    sums = sums + along_y(sums, 3)
    sums = sums + along_first(sums, 1) + along_first(sums, 2) + along_first(sums, 3)
    low = taken(after(near_one, sums), 0)
    high = taken(after(near_three, sums), 2 * ROWS)
    far_low = along_first(low, 3)
    far_high = along_first(high, 1)
    sums = after(sums, low, high)
    near_one, near_three = after(near_one, low, high), after(near_three, low, high)
    others = [sibling(v) for v in (after(mine, low, high), near_one, near_three)]
    sums = sums + sibling(after(sums, others[0]))
    new_weight, trust_step = apply_update(
        blocks,
        own_unit(0) + own_unit(1) + own_unit(3) + other_unit(0) + other_unit(1) + other_unit(3),
        sums,
        weight,
        [mine, near_one, near_three, *others],
        update,
        None,
    )
    far_low, far_high = after(far_low, new_weight), after(far_high, new_weight)
    far_others = [sibling(far_low), sibling(far_high)]
    (new_weight,) = apply_update(
        blocks, own_unit(2), sums, weight, [far_low, far_high], None, new_weight
    )
    (new_weight,) = apply_update(
        blocks, other_unit(2), sums, weight, far_others, None, new_weight
    )
    return (input_grad, new_weight, first_next, second_next, trust_step)


def solution(mesh):
    split = Mesh(mesh.devices.reshape(4, 4, 2, 4), ("x", "z", "c", "y"))
    rows = P(("y", "x", "z", "c"), None)
    return jax.shard_map(
        per_device,
        mesh=split,
        in_specs=(P(DP, "y"), P(DP, None), P("y", None), rows, rows),
        out_specs=(P(DP, "y"), P("y", None), rows, rows, rows),
        check_vma=False,
    )
```

```python
import jax
import jax.numpy as jnp
from jax import lax
from jax.experimental import pallas as pl
from jax.experimental.pallas import tpu as pltpu
from jax.sharding import Mesh
from jax.sharding import PartitionSpec as P

STEP = 1000
DP = ("x", "z", "c")
ROWS = 256
D = 512
VMEM = pl.BlockSpec(memory_space=pltpu.VMEM)
SMEM = pl.BlockSpec(memory_space=pltpu.SMEM)
HBM = pl.BlockSpec(memory_space=pltpu.HBM)
SHORT = pl.CostEstimate(flops=2**20, bytes_accessed=2**16, transcendentals=0)
LONG = pl.CostEstimate(flops=2**34, bytes_accessed=2**26, transcendentals=0)


def exchanges(axis, k):
    pairs = []
    for x in range(4):
        for z in range(4):
            for c in range(2):
                along_x = (axis == "first") == (c == 0)
                to_x, to_z = (x ^ k, z) if along_x else (x, z ^ k)
                pairs.append(((x * 4 + z) * 2 + c, (to_x * 4 + to_z) * 2 + c))
    return pairs


def along_first(value, k):
    return lax.ppermute(value, DP, exchanges("first", k))


def along_second(value, k):
    return lax.ppermute(value, DP, exchanges("second", k))


def along_y(value, k):
    return lax.ppermute(value, "y", [(y, y ^ k) for y in range(4)])


def sibling(value):
    return lax.ppermute(value, "c", [(0, 1), (1, 0)])


def in_hbm(value):
    return pltpu.with_memory_space_constraint(value, pltpu.HBM)


def in_vmem(value):
    return pltpu.with_memory_space_constraint(value, pltpu.VMEM)


def after(value, *others):
    return lax.optimization_barrier((value, *others))[0]


def first_body(picks, blocks, up_ref, pre_ref, out, up_t, columns, arrived, up, up_arrived):
    copies = []
    up_copy = pltpu.make_async_copy(up_ref, up, up_arrived)
    up_copy.start()
    for i, pick in enumerate(picks):
        start = pl.multiple_of(blocks[pick] * ROWS, ROWS)
        copies.append(
            pltpu.make_async_copy(
                pre_ref.at[:, pl.ds(start, ROWS)],
                columns.at[:, pl.ds(i * ROWS, ROWS)],
                arrived.at[i],
            )
        )
        copies[-1].start()
    up_copy.wait()
    up_t[...] = up[...].T
    zero = jnp.zeros((), jnp.bfloat16)
    for i, copy in enumerate(copies):
        copy.wait()
        out[i * D : (i + 1) * D, :] = jnp.dot(
            up_t[...],
            jnp.maximum(columns[:, i * ROWS : (i + 1) * ROWS], zero),
            preferred_element_type=jnp.float32,
        ).astype(jnp.bfloat16)


def first_terms(preactivation, upstream, blocks, picks):
    tokens = preactivation.shape[0]

    def body(*refs):
        first_body(picks, *refs)

    return pl.pallas_call(
        body,
        out_shape=(
            jax.ShapeDtypeStruct((len(picks) * D, ROWS), jnp.bfloat16),
            jax.ShapeDtypeStruct((D, tokens), jnp.bfloat16),
        ),
        in_specs=[SMEM, HBM, HBM],
        out_specs=(VMEM, VMEM),
        scratch_shapes=[
            pltpu.VMEM((tokens, len(picks) * ROWS), jnp.bfloat16),
            pltpu.SemaphoreType.DMA((len(picks),)),
            pltpu.VMEM(upstream.shape, upstream.dtype),
            pltpu.SemaphoreType.DMA,
        ],
        compiler_params=pltpu.CompilerParams(vmem_limit_bytes=16 * 2**20),
        cost_estimate=LONG,
        name="first_terms",
    )(blocks, in_hbm(upstream), in_hbm(preactivation))


def terms_body(picks, parts, adds, blocks, up_ref, pre_ref, *refs):
    ins, outs = refs[: sum(map(len, adds))], refs[sum(map(len, adds)) :]
    zero = jnp.zeros((), jnp.bfloat16)
    picks = list(picks)
    for part, offsets, out in zip(parts, adds, outs):
        mine, ins = ins[: len(offsets)], ins[len(offsets) :]
        for k in range(part):
            start = pl.multiple_of(blocks[picks.pop(0)] * ROWS, ROWS)
            total = jnp.dot(
                up_ref[...],
                jnp.maximum(pre_ref[:, pl.ds(start, ROWS)], zero),
                preferred_element_type=jnp.float32,
            )
            for ref, offset in zip(mine, offsets):
                begin = offset + k * D
                total = total + ref[begin : begin + D, :].astype(jnp.float32)
            out[k * D : (k + 1) * D, :] = total.astype(jnp.bfloat16)


def terms(preactivation, up_t, blocks, picks, parts, adds=None, cost=SHORT):
    adds = adds or [()] * len(parts)
    offsets = [[begin for _, begin in group] for group in adds]

    def body(*refs):
        terms_body(picks, parts, offsets, *refs)

    return pl.pallas_call(
        body,
        out_shape=tuple(jax.ShapeDtypeStruct((p * D, ROWS), jnp.bfloat16) for p in parts),
        in_specs=[SMEM, VMEM, VMEM] + [VMEM] * sum(map(len, adds)),
        out_specs=tuple(VMEM for _ in parts),
        compiler_params=pltpu.CompilerParams(vmem_limit_bytes=16 * 2**20),
        cost_estimate=cost,
        name="terms",
    )(blocks, up_t, in_vmem(preactivation), *(a for group in adds for a, _ in group))


WIDE = 2048


def back_body(lo, up_ref, pre_ref, weight_ref, *refs):
    here = pl.ds(pl.multiple_of((pl.program_id(0) + lo) * WIDE, WIDE), WIDE)
    back = lax.dot_general(
        up_ref[...], weight_ref[here, :], (((1,), (1,)), ((), ())), preferred_element_type=jnp.float32
    )
    refs[-1][...] = jnp.where(
        pre_ref[:, here] > 0, back.astype(jnp.bfloat16), jnp.zeros((), jnp.bfloat16)
    )


def back_columns(lo, count, upstream, preactivation, weight, before):
    extra = [] if before is None else [before]
    tokens = preactivation.shape[0]

    def body(*refs):
        back_body(lo, *refs)

    return pl.pallas_call(
        body,
        out_shape=jax.ShapeDtypeStruct(preactivation.shape, jnp.bfloat16),
        grid=(count,),
        in_specs=[VMEM, VMEM, VMEM]
        + [pl.BlockSpec(memory_space=pl.ANY)] * len(extra),
        out_specs=pl.BlockSpec((tokens, WIDE), lambda i: (0, i + lo)),
        input_output_aliases={3: 0} if extra else {},
        compiler_params=pltpu.CompilerParams(vmem_limit_bytes=24 * 2**20),
        cost_estimate=LONG,
        name="back_columns",
    )(upstream, in_vmem(preactivation), in_vmem(weight), *map(in_hbm, extra))


def update_body(
    block, g0, g1, g2, g3, g4, g5, first, second, weight,
    first_out, second_out, update_out, short_out,
):
    beta_one = 0.9
    beta_two = 0.999
    bias_one = 1.0 - beta_one**STEP
    bias_two = 1.0 - beta_two**STEP
    start = pl.multiple_of(block[0] * ROWS, ROWS)
    own = pl.ds(start, ROWS)
    update_sq = jnp.zeros((8, 128), jnp.float32)
    weight_sq = jnp.zeros((8, 128), jnp.float32)
    for j in range(D // 128):
        part = slice(j * 128, (j + 1) * 128)
        total = g0[part, :].astype(jnp.float32)
        for ref in (g1, g2, g3, g4, g5):
            total = total + ref[part, :].astype(jnp.float32)
        gradient = total.T
        first_next = beta_one * first[:, part] + (1.0 - beta_one) * gradient
        second_next = beta_two * second[:, part] + (1.0 - beta_two) * gradient * gradient
        own_weight = weight[own, part].astype(jnp.float32)
        update = (
            first_next * (1.0 / bias_one) / (jnp.sqrt(second_next * (1.0 / bias_two)) + 1e-06)
            + 0.02 * own_weight
        )
        first_out[:, part] = first_next
        second_out[:, part] = second_next
        update_out[:, part] = update
        short_out[0:ROWS, part] = update.astype(jnp.bfloat16)
        update_sq = update_sq + jnp.sum((update * update).reshape(ROWS // 8, 8, 128), axis=0)
        weight_sq = weight_sq + jnp.sum(
            (own_weight * own_weight).reshape(ROWS // 8, 8, 128), axis=0
        )
    norms = jnp.concatenate([update_sq, weight_sq])
    for j in range(3):
        piece = norms.astype(jnp.bfloat16)
        short_out[ROWS : ROWS + 16, j * 128 : (j + 1) * 128] = piece
        norms = norms - piece.astype(jnp.float32)
    short_out[ROWS : ROWS + 16, 384:512] = jnp.zeros((16, 128), jnp.bfloat16)


def update_rows(block, parts, first, second, weight):
    long = jax.ShapeDtypeStruct((ROWS, D), jnp.float32)
    return pl.pallas_call(
        update_body,
        out_shape=(
            long,
            long,
            long,
            jax.ShapeDtypeStruct((ROWS + 16, D), jnp.bfloat16),
        ),
        in_specs=[SMEM] + [VMEM] * 9,
        out_specs=(VMEM,) * 4,
        compiler_params=pltpu.CompilerParams(vmem_limit_bytes=16 * 2**20),
        cost_estimate=SHORT,
        name="update_rows",
    )(block, *parts, first, second, in_vmem(weight))


def apply_body(picks, sizes, trust, blocks, sums_ref, weight, *refs):
    updates = refs[: len(sizes)]
    ready, stored = refs[-2:]
    if trust:
        update_ref, out, trust_out = refs[len(sizes)], refs[-4], refs[-3]
    else:
        out = refs[-3]
    update_sq = jnp.sum(sums_ref[0:8, :], axis=(0, 1), keepdims=True)
    weight_sq = jnp.sum(sums_ref[8:16, :], axis=(0, 1), keepdims=True)
    ratio = jnp.sqrt(weight_sq) / jnp.sqrt(update_sq)
    step = (0.02 * ratio).astype(jnp.bfloat16)
    places = [(update, k) for size, update in zip(sizes, updates) for k in range(size)]
    stores = []
    for i, (update, k) in enumerate(places):
        begin = pl.multiple_of(blocks[picks[i]] * ROWS, ROWS)
        ready[i] = weight[pl.ds(begin, ROWS), :] - step * update[k * ROWS : (k + 1) * ROWS, :]
        stores.append(
            pltpu.make_async_copy(ready.at[i], out.at[pl.ds(begin, ROWS)], stored.at[i])
        )
        stores[-1].start()
    if trust:
        trust_out[...] = ratio * update_ref[...]
    for store in stores:
        store.wait()


def apply_update(blocks, picks, sums, weight, updates, update, before):
    sizes = [u.shape[0] // ROWS for u in updates]
    count = sum(sizes)
    trust = [] if update is None else [update]
    extra = [] if before is None else [before]

    def body(*refs):
        apply_body(picks, sizes, bool(trust), *refs)

    return pl.pallas_call(
        body,
        out_shape=(jax.ShapeDtypeStruct(weight.shape, jnp.bfloat16),)
        + tuple(jax.ShapeDtypeStruct(u.shape, u.dtype) for u in trust),
        in_specs=[SMEM, VMEM, VMEM] + [VMEM] * (len(updates) + len(trust)) + [HBM] * len(extra),
        out_specs=(HBM,) + (VMEM,) * len(trust),
        input_output_aliases={3 + len(updates) + len(trust): 0} if extra else {},
        scratch_shapes=[
            pltpu.VMEM((count, ROWS, D), jnp.bfloat16),
            pltpu.SemaphoreType.DMA((count,)),
        ],
        compiler_params=pltpu.CompilerParams(vmem_limit_bytes=16 * 2**20),
        cost_estimate=SHORT,
        name="apply_update",
    )(blocks, sums, in_vmem(weight), *updates, *trust, *map(in_hbm, extra))


def joined(*values):
    def body(*refs):
        rows_out, sums_out = refs[-2:]
        total = jnp.zeros((16, 128), jnp.float32)
        for k, ref in enumerate(refs[:-2]):
            rows_out[k * ROWS : (k + 1) * ROWS, :] = ref[0:ROWS, :]
            for j in range(3):
                total = total + ref[ROWS : ROWS + 16, j * 128 : (j + 1) * 128].astype(jnp.float32)
        sums_out[...] = total

    return pl.pallas_call(
        body,
        out_shape=(
            jax.ShapeDtypeStruct((len(values) * ROWS, D), jnp.bfloat16),
            jax.ShapeDtypeStruct((16, 128), jnp.float32),
        ),
        in_specs=[VMEM] * len(values),
        out_specs=(VMEM, VMEM),
        compiler_params=pltpu.CompilerParams(vmem_limit_bytes=16 * 2**20),
        cost_estimate=SHORT,
        name="joined",
    )(*values)


def taken(value, begin):
    rows = value.shape[0] // 2

    def body(ref, out):
        out[...] = ref[begin : begin + rows, :]

    return pl.pallas_call(
        body,
        out_shape=jax.ShapeDtypeStruct((rows, value.shape[1]), value.dtype),
        in_specs=[VMEM],
        out_specs=VMEM,
        compiler_params=pltpu.CompilerParams(vmem_limit_bytes=16 * 2**20),
        cost_estimate=SHORT,
        name="taken",
    )(value)


def added(*values):
    total = values[0].astype(jnp.float32)
    for value in values[1:]:
        total = total + value.astype(jnp.float32)
    return total.astype(jnp.bfloat16)


def own_unit(k):
    return [k * 4 + j for j in range(4)]


def other_unit(k):
    return [16 + k * 4 + j for j in range(4)]


def per_device(preactivation, upstream, weight, first_moment, second_moment):
    x, z, c = lax.axis_index("x"), lax.axis_index("z"), lax.axis_index("c")
    first = jnp.where(c == 0, x, z)
    second = jnp.where(c == 0, z, x)
    first_stride = jnp.where(c == 0, 8, 2)
    second_stride = jnp.where(c == 0, 2, 8)
    place = jnp.arange(32, dtype=jnp.int32)
    unit, member = (place >> 2) & 3, place & 3
    mine = place < 16
    on_first = first ^ jnp.where(mine, unit, member)
    on_second = second ^ jnp.where(mine, member, unit)
    blocks = on_first * first_stride + on_second * second_stride + jnp.where(mine, c, 1 - c)

    near_free = lambda unit: unit(1)[:2] + unit(3)[2:]
    near_late = lambda unit: unit(1)[2:] + unit(3)[:2]

    send_far, up_t = first_terms(preactivation, upstream, blocks, other_unit(2))

    def part(picks, parts, adds=None, then=(), cost=SHORT):
        return terms(preactivation, after(up_t, *then), blocks, picks, parts, adds, cost)

    got_far = sibling(send_far)
    keep_far = part(own_unit(2), (2, 2), then=(send_far,), cost=LONG)
    half = 2 * D
    (send_free,) = part(near_free(other_unit), (4,), then=keep_far)
    keep_far = [after(v, send_free) for v in keep_far]
    far_low = added(keep_far[0], got_far[:half])
    far_high = added(keep_far[1], got_far[half:])
    from_one = along_first(far_low, 1)
    from_three = along_first(far_high, 3)

    got_free = sibling(send_free)
    (send_late,) = part(near_late(other_unit), (4,), then=(far_low, far_high), cost=LONG)
    got_late = sibling(send_late)
    one_low, three_high = part(
        near_free(own_unit), (2, 2), [[(got_free, 0)], [(got_free, half)]], then=(send_late,)
    )
    sum_one_low = along_first(one_low, 1)
    sum_three_high = along_first(three_high, 3)
    (send_here,) = part(other_unit(0), (4,), then=(one_low, three_high), cost=LONG)
    got_here = sibling(send_here)
    one_high, three_low = part(
        near_late(own_unit),
        (2, 2),
        [[(got_late, 0), (from_three, 0)], [(got_late, half), (from_one, 0)]],
        then=(send_here,),
    )
    sum_one_high = along_first(one_high, 1)
    sum_three_low = along_first(three_low, 3)
    input_grad = back_columns(
        0, 2, after(upstream, one_high, three_low), preactivation, weight, None
    )
    (here,) = part(own_unit(0), (4,), [[(got_here, 0)]], then=(input_grad,))
    near = (
        added(here[D:half], sum_one_low[D:], sum_three_low[D:]),
        added(here[half : half + D], sum_one_high[:D], sum_three_high[:D]),
        added(here[half + D :], sum_one_high[D:], sum_three_high[D:]),
    )
    got = [along_second(v, k) for v, k in zip(near, (1, 2, 3))]
    input_grad = back_columns(2, 2, after(upstream, *near), preactivation, weight, input_grad)
    first_next, second_next, update, short = update_rows(
        blocks,
        [here, sum_one_low, sum_three_low, *got],
        first_moment,
        second_moment,
        after(weight, input_grad),
    )

    mine, sums = joined(short, *(along_second(short, k) for k in (1, 2, 3)))
    near_one = along_first(mine, 1)
    near_three = along_first(mine, 3)
    sums = sums + along_y(sums, 1)
    sums = sums + along_y(sums, 3)
    sums = sums + along_first(sums, 1) + along_first(sums, 2) + along_first(sums, 3)
    low = taken(after(near_one, sums), 0)
    high = taken(after(near_three, sums), 2 * ROWS)
    far_low = along_first(low, 3)
    far_high = along_first(high, 1)
    sums = after(sums, low, high)
    near_one, near_three = after(near_one, low, high), after(near_three, low, high)
    others = [sibling(v) for v in (after(mine, low, high), near_one, near_three)]
    sums = sums + sibling(after(sums, others[0]))
    new_weight, trust_step = apply_update(
        blocks,
        own_unit(0) + own_unit(1) + own_unit(3) + other_unit(0) + other_unit(1) + other_unit(3),
        sums,
        weight,
        [mine, near_one, near_three, *others],
        update,
        None,
    )
    far_low, far_high = after(far_low, new_weight), after(far_high, new_weight)
    (new_weight,) = apply_update(
        blocks,
        own_unit(2) + other_unit(2),
        sums,
        weight,
        [far_low, far_high, sibling(far_low), sibling(far_high)],
        None,
        new_weight,
    )
    return (input_grad, new_weight, first_next, second_next, trust_step)


def solution(mesh):
    split = Mesh(mesh.devices.reshape(4, 4, 2, 4), ("x", "z", "c", "y"))
    rows = P(("y", "x", "z", "c"), None)
    return jax.shard_map(
        per_device,
        mesh=split,
        in_specs=(P(DP, "y"), P(DP, None), P("y", None), rows, rows),
        out_specs=(P(DP, "y"), P("y", None), rows, rows, rows),
        check_vma=False,
    )
```

```python
import jax
import jax.numpy as jnp
from jax import lax
from jax.experimental import pallas as pl
from jax.experimental.pallas import tpu as pltpu
from jax.sharding import Mesh
from jax.sharding import PartitionSpec as P

STEP = 1000
DP = ("x", "z", "c")
ROWS = 256
D = 512
VMEM = pl.BlockSpec(memory_space=pltpu.VMEM)
SMEM = pl.BlockSpec(memory_space=pltpu.SMEM)
HBM = pl.BlockSpec(memory_space=pltpu.HBM)
SHORT = pl.CostEstimate(flops=2**20, bytes_accessed=2**16, transcendentals=0)
LONG = pl.CostEstimate(flops=2**34, bytes_accessed=2**26, transcendentals=0)


def exchanges(axis, k):
    pairs = []
    for x in range(4):
        for z in range(4):
            for c in range(2):
                along_x = (axis == "first") == (c == 0)
                to_x, to_z = (x ^ k, z) if along_x else (x, z ^ k)
                pairs.append(((x * 4 + z) * 2 + c, (to_x * 4 + to_z) * 2 + c))
    return pairs


def along_first(value, k):
    return lax.ppermute(value, DP, exchanges("first", k))


def along_second(value, k):
    return lax.ppermute(value, DP, exchanges("second", k))


def along_y(value, k):
    return lax.ppermute(value, "y", [(y, y ^ k) for y in range(4)])


def sibling(value):
    return lax.ppermute(value, "c", [(0, 1), (1, 0)])


def in_hbm(value):
    return pltpu.with_memory_space_constraint(value, pltpu.HBM)


def in_vmem(value):
    return pltpu.with_memory_space_constraint(value, pltpu.VMEM)


def after(value, *others):
    return lax.optimization_barrier((value, *others))[0]


def first_body(picks, blocks, up_ref, pre_ref, out, up_t, columns, arrived, up, up_arrived):
    copies = []
    up_copy = pltpu.make_async_copy(up_ref, up, up_arrived)
    up_copy.start()
    for i, pick in enumerate(picks):
        start = pl.multiple_of(blocks[pick] * ROWS, ROWS)
        copies.append(
            pltpu.make_async_copy(
                pre_ref.at[:, pl.ds(start, ROWS)],
                columns.at[:, pl.ds(i * ROWS, ROWS)],
                arrived.at[i],
            )
        )
        copies[-1].start()
    up_copy.wait()
    up_t[...] = up[...].T
    zero = jnp.zeros((), jnp.bfloat16)
    for i, copy in enumerate(copies):
        copy.wait()
        out[i * D : (i + 1) * D, :] = jnp.dot(
            up_t[...],
            jnp.maximum(columns[:, i * ROWS : (i + 1) * ROWS], zero),
            preferred_element_type=jnp.float32,
        ).astype(jnp.bfloat16)


def first_terms(preactivation, upstream, blocks, picks):
    tokens = preactivation.shape[0]

    def body(*refs):
        first_body(picks, *refs)

    return pl.pallas_call(
        body,
        out_shape=(
            jax.ShapeDtypeStruct((len(picks) * D, ROWS), jnp.bfloat16),
            jax.ShapeDtypeStruct((D, tokens), jnp.bfloat16),
        ),
        in_specs=[SMEM, HBM, HBM],
        out_specs=(VMEM, VMEM),
        scratch_shapes=[
            pltpu.VMEM((tokens, len(picks) * ROWS), jnp.bfloat16),
            pltpu.SemaphoreType.DMA((len(picks),)),
            pltpu.VMEM(upstream.shape, upstream.dtype),
            pltpu.SemaphoreType.DMA,
        ],
        compiler_params=pltpu.CompilerParams(vmem_limit_bytes=16 * 2**20),
        cost_estimate=LONG,
        name="first_terms",
    )(blocks, in_hbm(upstream), in_hbm(preactivation))


def terms_body(picks, parts, adds, blocks, up_ref, pre_ref, *refs):
    ins, outs = refs[: sum(map(len, adds))], refs[sum(map(len, adds)) :]
    zero = jnp.zeros((), jnp.bfloat16)
    picks = list(picks)
    for part, offsets, out in zip(parts, adds, outs):
        mine, ins = ins[: len(offsets)], ins[len(offsets) :]
        for k in range(part):
            start = pl.multiple_of(blocks[picks.pop(0)] * ROWS, ROWS)
            total = jnp.dot(
                up_ref[...],
                jnp.maximum(pre_ref[:, pl.ds(start, ROWS)], zero),
                preferred_element_type=jnp.float32,
            )
            for ref, offset in zip(mine, offsets):
                begin = offset + k * D
                total = total + ref[begin : begin + D, :].astype(jnp.float32)
            out[k * D : (k + 1) * D, :] = total.astype(jnp.bfloat16)


def terms(preactivation, up_t, blocks, picks, parts, adds=None, cost=SHORT):
    adds = adds or [()] * len(parts)
    offsets = [[begin for _, begin in group] for group in adds]

    def body(*refs):
        terms_body(picks, parts, offsets, *refs)

    return pl.pallas_call(
        body,
        out_shape=tuple(jax.ShapeDtypeStruct((p * D, ROWS), jnp.bfloat16) for p in parts),
        in_specs=[SMEM, VMEM, VMEM] + [VMEM] * sum(map(len, adds)),
        out_specs=tuple(VMEM for _ in parts),
        compiler_params=pltpu.CompilerParams(vmem_limit_bytes=16 * 2**20),
        cost_estimate=cost,
        name="terms",
    )(blocks, up_t, in_vmem(preactivation), *(a for group in adds for a, _ in group))


WIDE = 2048


def back_body(lo, up_ref, pre_ref, weight_ref, *refs):
    here = pl.ds(pl.multiple_of((pl.program_id(0) + lo) * WIDE, WIDE), WIDE)
    back = lax.dot_general(
        up_ref[...], weight_ref[here, :], (((1,), (1,)), ((), ())), preferred_element_type=jnp.float32
    )
    refs[-1][...] = jnp.where(
        pre_ref[:, here] > 0, back.astype(jnp.bfloat16), jnp.zeros((), jnp.bfloat16)
    )


def back_columns(lo, count, upstream, preactivation, weight, before):
    extra = [] if before is None else [before]
    tokens = preactivation.shape[0]

    def body(*refs):
        back_body(lo, *refs)

    return pl.pallas_call(
        body,
        out_shape=jax.ShapeDtypeStruct(preactivation.shape, jnp.bfloat16),
        grid=(count,),
        in_specs=[VMEM, VMEM, VMEM]
        + [pl.BlockSpec(memory_space=pl.ANY)] * len(extra),
        out_specs=pl.BlockSpec((tokens, WIDE), lambda i: (0, i + lo)),
        input_output_aliases={3: 0} if extra else {},
        compiler_params=pltpu.CompilerParams(vmem_limit_bytes=24 * 2**20),
        cost_estimate=LONG,
        name="back_columns",
    )(upstream, in_vmem(preactivation), in_vmem(weight), *map(in_hbm, extra))


def update_body(
    block, g0, g1, g2, g3, g4, g5, first, second, weight,
    first_out, second_out, update_out, short_out,
):
    beta_one = 0.9
    beta_two = 0.999
    bias_one = 1.0 - beta_one**STEP
    bias_two = 1.0 - beta_two**STEP
    start = pl.multiple_of(block[0] * ROWS, ROWS)
    own = pl.ds(start, ROWS)
    update_sq = jnp.zeros((8, 128), jnp.float32)
    weight_sq = jnp.zeros((8, 128), jnp.float32)
    for j in range(D // 128):
        part = slice(j * 128, (j + 1) * 128)
        total = g0[part, :].astype(jnp.float32)
        for ref in (g1, g2, g3, g4, g5):
            total = total + ref[part, :].astype(jnp.float32)
        gradient = total.T
        first_next = beta_one * first[:, part] + (1.0 - beta_one) * gradient
        second_next = beta_two * second[:, part] + (1.0 - beta_two) * gradient * gradient
        own_weight = weight[own, part].astype(jnp.float32)
        update = (
            first_next * (1.0 / bias_one) / (jnp.sqrt(second_next * (1.0 / bias_two)) + 1e-06)
            + 0.02 * own_weight
        )
        first_out[:, part] = first_next
        second_out[:, part] = second_next
        update_out[:, part] = update
        short_out[0:ROWS, part] = update.astype(jnp.bfloat16)
        update_sq = update_sq + jnp.sum((update * update).reshape(ROWS // 8, 8, 128), axis=0)
        weight_sq = weight_sq + jnp.sum(
            (own_weight * own_weight).reshape(ROWS // 8, 8, 128), axis=0
        )
    norms = jnp.concatenate([update_sq, weight_sq])
    for j in range(3):
        piece = norms.astype(jnp.bfloat16)
        short_out[ROWS : ROWS + 16, j * 128 : (j + 1) * 128] = piece
        norms = norms - piece.astype(jnp.float32)
    short_out[ROWS : ROWS + 16, 384:512] = jnp.zeros((16, 128), jnp.bfloat16)


def update_rows(block, parts, first, second, weight):
    long = jax.ShapeDtypeStruct((ROWS, D), jnp.float32)
    return pl.pallas_call(
        update_body,
        out_shape=(
            long,
            long,
            long,
            jax.ShapeDtypeStruct((ROWS + 16, D), jnp.bfloat16),
        ),
        in_specs=[SMEM] + [VMEM] * 9,
        out_specs=(VMEM,) * 4,
        compiler_params=pltpu.CompilerParams(vmem_limit_bytes=16 * 2**20),
        cost_estimate=SHORT,
        name="update_rows",
    )(block, *parts, first, second, in_vmem(weight))


def apply_body(picks, sizes, trust, blocks, sums_ref, weight, *refs):
    updates = refs[: len(sizes)]
    ready, stored = refs[-2:]
    if trust:
        update_ref, out, trust_out = refs[len(sizes)], refs[-4], refs[-3]
    else:
        out = refs[-3]
    update_sq = jnp.sum(sums_ref[0:8, :], axis=(0, 1), keepdims=True)
    weight_sq = jnp.sum(sums_ref[8:16, :], axis=(0, 1), keepdims=True)
    ratio = jnp.sqrt(weight_sq) / jnp.sqrt(update_sq)
    step = (0.02 * ratio).astype(jnp.bfloat16)
    places = [(update, k) for size, update in zip(sizes, updates) for k in range(size)]
    stores = []
    for i, (update, k) in enumerate(places):
        begin = pl.multiple_of(blocks[picks[i]] * ROWS, ROWS)
        ready[i] = weight[pl.ds(begin, ROWS), :] - step * update[k * ROWS : (k + 1) * ROWS, :]
        stores.append(
            pltpu.make_async_copy(ready.at[i], out.at[pl.ds(begin, ROWS)], stored.at[i])
        )
        stores[-1].start()
    if trust:
        trust_out[...] = ratio * update_ref[...]
    for store in stores:
        store.wait()


def apply_update(blocks, picks, sums, weight, updates, update, before):
    sizes = [u.shape[0] // ROWS for u in updates]
    count = sum(sizes)
    trust = [] if update is None else [update]
    extra = [] if before is None else [before]

    def body(*refs):
        apply_body(picks, sizes, bool(trust), *refs)

    return pl.pallas_call(
        body,
        out_shape=(jax.ShapeDtypeStruct(weight.shape, jnp.bfloat16),)
        + tuple(jax.ShapeDtypeStruct(u.shape, u.dtype) for u in trust),
        in_specs=[SMEM, VMEM, VMEM] + [VMEM] * (len(updates) + len(trust)) + [HBM] * len(extra),
        out_specs=(HBM,) + (VMEM,) * len(trust),
        input_output_aliases={3 + len(updates) + len(trust): 0} if extra else {},
        scratch_shapes=[
            pltpu.VMEM((count, ROWS, D), jnp.bfloat16),
            pltpu.SemaphoreType.DMA((count,)),
        ],
        compiler_params=pltpu.CompilerParams(vmem_limit_bytes=16 * 2**20),
        cost_estimate=SHORT,
        name="apply_update",
    )(blocks, sums, in_vmem(weight), *updates, *trust, *map(in_hbm, extra))


def joined(*values):
    def body(*refs):
        rows_out, sums_out = refs[-2:]
        total = jnp.zeros((16, 128), jnp.float32)
        for k, ref in enumerate(refs[:-2]):
            rows_out[k * ROWS : (k + 1) * ROWS, :] = ref[0:ROWS, :]
            for j in range(3):
                total = total + ref[ROWS : ROWS + 16, j * 128 : (j + 1) * 128].astype(jnp.float32)
        sums_out[...] = total

    return pl.pallas_call(
        body,
        out_shape=(
            jax.ShapeDtypeStruct((len(values) * ROWS, D), jnp.bfloat16),
            jax.ShapeDtypeStruct((16, 128), jnp.float32),
        ),
        in_specs=[VMEM] * len(values),
        out_specs=(VMEM, VMEM),
        compiler_params=pltpu.CompilerParams(vmem_limit_bytes=16 * 2**20),
        cost_estimate=SHORT,
        name="joined",
    )(*values)


def taken(value, begin):
    rows = value.shape[0] // 2

    def body(ref, out):
        out[...] = ref[begin : begin + rows, :]

    return pl.pallas_call(
        body,
        out_shape=jax.ShapeDtypeStruct((rows, value.shape[1]), value.dtype),
        in_specs=[VMEM],
        out_specs=VMEM,
        compiler_params=pltpu.CompilerParams(vmem_limit_bytes=16 * 2**20),
        cost_estimate=SHORT,
        name="taken",
    )(value)


def added(*values):
    total = values[0].astype(jnp.float32)
    for value in values[1:]:
        total = total + value.astype(jnp.float32)
    return total.astype(jnp.bfloat16)


def own_unit(k):
    return [k * 4 + j for j in range(4)]


def other_unit(k):
    return [16 + k * 4 + j for j in range(4)]


def per_device(preactivation, upstream, weight, first_moment, second_moment):
    x, z, c = lax.axis_index("x"), lax.axis_index("z"), lax.axis_index("c")
    first = jnp.where(c == 0, x, z)
    second = jnp.where(c == 0, z, x)
    first_stride = jnp.where(c == 0, 8, 2)
    second_stride = jnp.where(c == 0, 2, 8)
    place = jnp.arange(32, dtype=jnp.int32)
    unit, member = (place >> 2) & 3, place & 3
    mine = place < 16
    on_first = first ^ jnp.where(mine, unit, member)
    on_second = second ^ jnp.where(mine, member, unit)
    blocks = on_first * first_stride + on_second * second_stride + jnp.where(mine, c, 1 - c)

    near_free = lambda unit: unit(1)[:2] + unit(3)[2:]
    near_late = lambda unit: unit(1)[2:] + unit(3)[:2]

    send_far, up_t = first_terms(preactivation, upstream, blocks, other_unit(2))

    def part(picks, parts, adds=None, then=(), cost=SHORT):
        return terms(preactivation, after(up_t, *then), blocks, picks, parts, adds, cost)

    got_far = sibling(send_far)
    keep_far = part(own_unit(2), (2, 2), then=(send_far,), cost=LONG)
    half = 2 * D
    (send_free,) = part(near_free(other_unit), (4,), then=keep_far)
    keep_far = [after(v, send_free) for v in keep_far]
    far_low = added(keep_far[0], got_far[:half])
    far_high = added(keep_far[1], got_far[half:])
    from_one = along_first(far_low, 1)
    from_three = along_first(far_high, 3)

    got_free = sibling(send_free)
    (send_late,) = part(near_late(other_unit), (4,), then=(far_low, far_high), cost=LONG)
    got_late = sibling(send_late)
    one_low, three_high = part(
        near_free(own_unit), (2, 2), [[(got_free, 0)], [(got_free, half)]], then=(send_late,)
    )
    sum_one_low = along_first(one_low, 1)
    sum_three_high = along_first(three_high, 3)
    (send_here,) = part(other_unit(0), (4,), then=(one_low, three_high), cost=LONG)
    got_here = sibling(send_here)
    one_high, three_low = part(
        near_late(own_unit),
        (2, 2),
        [[(got_late, 0), (from_three, 0)], [(got_late, half), (from_one, 0)]],
        then=(send_here,),
    )
    sum_one_high = along_first(one_high, 1)
    sum_three_low = along_first(three_low, 3)
    input_grad = back_columns(
        0, 2, after(upstream, one_high, three_low), preactivation, weight, None
    )
    (here,) = part(own_unit(0), (4,), [[(got_here, 0)]], then=(input_grad,))
    near = (
        added(here[D:half], sum_one_low[D:], sum_three_low[D:]),
        added(here[half : half + D], sum_one_high[:D], sum_three_high[:D]),
        added(here[half + D :], sum_one_high[D:], sum_three_high[D:]),
    )
    got = [along_second(v, k) for v, k in zip(near, (1, 2, 3))]
    input_grad = back_columns(2, 2, after(upstream, *near), preactivation, weight, input_grad)
    first_next, second_next, update, short = update_rows(
        blocks,
        [here, sum_one_low, sum_three_low, *got],
        first_moment,
        second_moment,
        after(weight, input_grad),
    )

    mine, sums = joined(short, *(along_second(short, k) for k in (1, 2, 3)))
    near_one = along_first(mine, 1)
    near_three = along_first(mine, 3)
    sums = sums + along_y(sums, 1)
    sums = sums + along_y(sums, 2)
    sums = sums + along_first(sums, 1) + along_first(sums, 2) + along_first(sums, 3)
    low = taken(after(near_one, sums), 0)
    high = taken(after(near_three, sums), 2 * ROWS)
    far_low = along_first(low, 3)
    far_high = along_first(high, 1)
    sums = after(sums, low, high)
    near_one, near_three = after(near_one, low, high), after(near_three, low, high)
    others = [sibling(v) for v in (after(mine, low, high), near_one, near_three)]
    sums = sums + sibling(after(sums, others[0]))
    new_weight, trust_step = apply_update(
        blocks,
        own_unit(0) + own_unit(1) + own_unit(3) + other_unit(0) + other_unit(1) + other_unit(3),
        sums,
        weight,
        [mine, near_one, near_three, *others],
        update,
        None,
    )
    far_low, far_high = after(far_low, new_weight), after(far_high, new_weight)
    (new_weight,) = apply_update(
        blocks,
        own_unit(2) + other_unit(2),
        sums,
        weight,
        [far_low, far_high, sibling(far_low), sibling(far_high)],
        None,
        new_weight,
    )
    return (input_grad, new_weight, first_next, second_next, trust_step)


def solution(mesh):
    split = Mesh(mesh.devices.reshape(4, 4, 2, 4), ("x", "z", "c", "y"))
    rows = P(("y", "x", "z", "c"), None)
    return jax.shard_map(
        per_device,
        mesh=split,
        in_specs=(P(DP, "y"), P(DP, None), P("y", None), rows, rows),
        out_specs=(P(DP, "y"), P("y", None), rows, rows, rows),
        check_vma=False,
    )
```
